512 devices in a mesh: ctx: 64 (over z, x), tp: 8 (over y, core).
Axes of the slice: x: 4, y: 4, z: 16, core: 2. Of those that a mesh axis runs over, the one named last changes fastest.
Arguments:
- query_rows: bfloat16 [24576, 2048], P('ctx', 'tp'), may hold values from -24 to 24
- key_rows: bfloat16 [24576, 1024], P('ctx', 'tp'), may hold values from -6 to 6
- value_rows: bfloat16 [24576, 1024], P('ctx', 'tp'), may hold values from -6 to 6
- grad_out: bfloat16 [24576, 4608], P('ctx', 'tp'), may hold values from -6 to 6
- out_weight: bfloat16 [2048, 4608], P('tp'), may hold values from -0.125 to 0.125
- doc_lengths: int32 [18], replicated, may hold values from 1 to 2689, 24576 in all
- doc_order: int32 [18], replicated, may hold values from 0 to 17, each once
Outputs:
- query_grads: bfloat16 [24576, 2048], P('ctx', 'tp')
- key_grads: bfloat16 [24576, 1024], P('ctx', 'tp')
- value_grads: bfloat16 [24576, 1024], P('ctx', 'tp')
The draws below stay inside these ranges and needn't reach their ends.
Inputs may be any that keep to these rules, and one draw needn't show every extreme that they name: `doc_lengths`: the lengths sum to 24576; the longest has exactly 2689 tokens. `doc_order`: each of 0 to 17 appears once.
All inputs are finite; a program needn't handle non-finite values.
Results may differ from the reference program's by a relative error of at most 0.012.
Values may be sent and summed in bfloat16 or wider, within the bound.
No kernel may reach another device: no remote copies, remote signals or barrier semaphores. Data moves between devices by JAX's collectives and lax.ppermute only.
A program may use at most 64 MiB of HBM per device.

```python
import math
import jax
import jax.numpy as jnp
import numpy as np
from jax import lax

D = 4608
HD = 128
QH_DEV = 2
TOK_DEV = 384
HEADS = 16
KV_HEADS = 8
TOKENS = 24576
REACH = 7
MAXDOC = 2689
NDOCS = 18


def shard_levels(stream_key, shape, cuts, low, high):
    level, own = 1.0, jax.random.fold_in(stream_key, 6)
    for axis_at, parts in cuts:
        draws = jnp.exp(jax.random.uniform(jax.random.fold_in(own, axis_at), (parts,), jnp.float32, low / len(cuts), high / len(cuts)))
        level = level * jnp.repeat(draws, shape[axis_at] // parts).reshape([-1 if axis == axis_at else 1 for axis in range(len(shape))])
    return level


def length_profile(count, total, bound, skew):
    weights = [(1 << 20) // math.isqrt(standing ** skew) + 1 for standing in range(2, count + 1)]
    rest, holding = total - bound - (count - 1), [1] * (count - 1)
    while rest > 0:
        candidates = [i for i in range(count - 1) if holding[i] < bound]
        whole, budget = sum([weights[i] for i in candidates]), rest
        for i in candidates:
            extra = min(bound - holding[i], max(1, budget * weights[i] // whole), rest)
            holding[i] = holding[i] + extra
            rest = rest - extra
    return np.array([bound] + holding)


def uneven(rng, count, total, most, lean):
    if count == 2:
        one = jax.random.randint(rng, (), max(1, total - most), min(most, total - 1) + 1)
        return jnp.stack([one, total - one])
    lengths = jnp.asarray(length_profile(count, total, most, lean), jnp.int32)
    pairs = (count - 1) // 2
    source_of, sink = lengths[1:1 + 2 * pairs:2], lengths[2:2 + 2 * pairs:2]
    slack = jnp.minimum(source_of - 1, most - sink)
    moved = jax.random.randint(jax.random.fold_in(rng, 1), (pairs,), 0, 1 << 20) % (slack + 1)
    lengths = lengths.at[1:1 + 2 * pairs:2].set(source_of - moved).at[2:2 + 2 * pairs:2].set(sink + moved)
    return lengths[jax.random.permutation(jax.random.fold_in(rng, 2), count)]


def bell_draw(stream_key, dims, scale, limit, pieces=(), kind=jnp.bfloat16):
    result = jax.random.normal(stream_key, dims, jnp.float32) * scale
    if len(pieces) > 0:
        result = shard_levels(stream_key, dims, pieces, -0.22, 0.18) * result
    return jnp.clip(result, min=-limit, max=limit).astype(kind)


def setup_inputs(seed: int = 0) -> dict:
    key_of = jax.random.split(jax.random.key(seed), 8)
    return {
        "query_rows": bell_draw(key_of[0], (TOKENS, HEADS * HD), 4.0, 24.0, ((0, 64), (1, 8))),
        "key_rows": bell_draw(key_of[1], (TOKENS, KV_HEADS * HD), 1.0, 6.0, ((0, 64), (1, 8))),
        "value_rows": bell_draw(key_of[2], (TOKENS, KV_HEADS * HD), 1.0, 6.0, ((0, 64), (1, 8))),
        "grad_out": bell_draw(key_of[3], (TOKENS, D), 1.0, 6.0, ((0, 64), (1, 8))),
        "out_weight": bell_draw(key_of[4], (HEADS * HD, D), (HEADS * HD) ** -0.5, 0.125, ((0, 8),)),
        "doc_lengths": uneven(key_of[5], NDOCS, TOKENS, MAXDOC, 1).astype(jnp.int32),
        "doc_order": jax.random.permutation(key_of[6], NDOCS).astype(jnp.int32),
    }


SOFT_CAP = 50.0
SCORE_SCALE = 1.0 / 12.0


def doc_index(places, doc_lengths, doc_order):
    numbers = jnp.arange(doc_lengths.shape[0], dtype=jnp.int32)
    picked = (doc_order[:, None] == numbers[None, :]).astype(jnp.int32)
    ordered = jnp.sum(picked * doc_lengths[None, :], axis=1, dtype=jnp.int32)
    bounds = jnp.cumsum(ordered, dtype=jnp.int32)
    return jnp.sum((places[:, None] >= bounds[None, :]).astype(jnp.int32), axis=1, dtype=jnp.int32)


def visible_pairs(query_places, key_places, query_docs, key_docs):
    same_doc = query_docs[:, None] == key_docs[None, :]
    causal = key_places[None, :] <= query_places[:, None]
    return same_doc & causal & (key_places[None, :] >= 0)


def capped_scores(query_block, key_block):
    raw_scores = jnp.einsum("qhe,khe->hqk", query_block.astype(jnp.float32), key_block.astype(jnp.float32))
    return SOFT_CAP * jnp.tanh(raw_scores * (SCORE_SCALE / SOFT_CAP))


def slopes_of(probs, scores, dprob, deltas):
    ratio = scores / SOFT_CAP
    return (probs * (dprob - deltas[:, :, None]) * (1.0 - ratio * ratio) * SCORE_SCALE).astype(jnp.bfloat16)


def widen(block):
    return jnp.repeat(block, QH_DEV, axis=1)


def reference(query_rows, key_rows, value_rows, grad_out, out_weight, doc_lengths, doc_order):
    head_grads = jnp.dot(grad_out, out_weight.T, preferred_element_type=jnp.float32).astype(jnp.bfloat16)
    queries = query_rows.reshape(TOKENS, HEADS, HD)
    keys_all = key_rows.reshape(TOKENS, KV_HEADS, HD)
    values_all = value_rows.reshape(TOKENS, KV_HEADS, HD)
    grad_heads = head_grads.reshape(TOKENS, HEADS, HD)
    margin = REACH * TOK_DEV
    window_rows = (REACH + 1) * TOK_DEV
    block_total = TOKENS // TOK_DEV
    front_zeros = jnp.zeros((margin, KV_HEADS, HD), key_rows.dtype)
    keys_padded = jnp.concatenate([front_zeros, keys_all], axis=0)
    values_padded = jnp.concatenate([front_zeros, values_all], axis=0)

    def query_block(block_number):
        first_row = block_number * TOK_DEV
        query_places = first_row + jnp.arange(TOK_DEV, dtype=jnp.int32)
        key_places = first_row - margin + jnp.arange(window_rows, dtype=jnp.int32)
        visible = visible_pairs(query_places, key_places, doc_index(query_places, doc_lengths, doc_order), doc_index(key_places, doc_lengths, doc_order))
        block_queries = lax.dynamic_slice_in_dim(queries, first_row, TOK_DEV, 0)
        block_grads = lax.dynamic_slice_in_dim(grad_heads, first_row, TOK_DEV, 0)
        block_keys = widen(lax.dynamic_slice_in_dim(keys_padded, first_row, window_rows, 0))
        block_values = widen(lax.dynamic_slice_in_dim(values_padded, first_row, window_rows, 0))
        scores = capped_scores(block_queries, block_keys)
        exponentials = jnp.where(visible[None], jnp.exp(scores), 0.0)
        exp_sums = jnp.sum(exponentials, axis=2)
        weights = exponentials.astype(jnp.bfloat16)
        accum = jnp.einsum("hqk,khe->qhe", weights.astype(jnp.float32), block_values.astype(jnp.float32))
        attended = accum / exp_sums.T[:, :, None]
        deltas = jnp.sum(block_grads.astype(jnp.float32) * attended, axis=2).T
        log_sums = jnp.log(exp_sums)
        probs = jnp.where(visible[None], jnp.exp(scores - log_sums[:, :, None]), 0.0)
        dprob = jnp.einsum("qhe,khe->hqk", block_grads.astype(jnp.float32), block_values.astype(jnp.float32))
        slopes = slopes_of(probs, scores, dprob, deltas)
        grads_q = jnp.einsum("hqk,khe->qhe", slopes.astype(jnp.float32), block_keys.astype(jnp.float32))
        return grads_q.astype(jnp.bfloat16), log_sums, deltas

    query_parts, log_parts, delta_parts = lax.map(query_block, jnp.arange(block_total, dtype=jnp.int32))
    query_grads = query_parts.reshape(TOKENS, HEADS * HD)
    log_sums_all = jnp.transpose(log_parts, (1, 0, 2)).reshape(HEADS, TOKENS)
    deltas_all = jnp.transpose(delta_parts, (1, 0, 2)).reshape(HEADS, TOKENS)
    back_zeros = jnp.zeros((margin, HEADS, HD), query_rows.dtype)
    queries_padded = jnp.concatenate([queries, back_zeros], axis=0)
    grads_padded = jnp.concatenate([grad_heads, back_zeros.astype(grad_heads.dtype)], axis=0)
    logs_padded = jnp.concatenate([log_sums_all, jnp.zeros((HEADS, margin), jnp.float32)], axis=1)
    deltas_padded = jnp.concatenate([deltas_all, jnp.zeros((HEADS, margin), jnp.float32)], axis=1)

    def key_block(block_number):
        first_row = block_number * TOK_DEV
        key_places = first_row + jnp.arange(TOK_DEV, dtype=jnp.int32)
        query_places = first_row + jnp.arange(window_rows, dtype=jnp.int32)
        visible = visible_pairs(query_places, key_places, doc_index(query_places, doc_lengths, doc_order), doc_index(key_places, doc_lengths, doc_order))
        block_queries = lax.dynamic_slice_in_dim(queries_padded, first_row, window_rows, 0)
        block_grads = lax.dynamic_slice_in_dim(grads_padded, first_row, window_rows, 0)
        block_logs = lax.dynamic_slice_in_dim(logs_padded, first_row, window_rows, 1)
        block_deltas = lax.dynamic_slice_in_dim(deltas_padded, first_row, window_rows, 1)
        block_keys = widen(lax.dynamic_slice_in_dim(keys_all, first_row, TOK_DEV, 0))
        block_values = widen(lax.dynamic_slice_in_dim(values_all, first_row, TOK_DEV, 0))
        scores = capped_scores(block_queries, block_keys)
        probs = jnp.where(visible[None], jnp.exp(scores - block_logs[:, :, None]), 0.0)
        dprob = jnp.einsum("qhe,khe->hqk", block_grads.astype(jnp.float32), block_values.astype(jnp.float32))
        slopes = slopes_of(probs, scores, dprob, block_deltas)
        grads_k = jnp.einsum("hqk,qhe->khe", slopes.astype(jnp.float32), block_queries.astype(jnp.float32))
        probs_low = probs.astype(jnp.bfloat16)
        grads_v = jnp.einsum("hqk,qhe->khe", probs_low.astype(jnp.float32), block_grads.astype(jnp.float32))
        grads_k = jnp.sum(grads_k.reshape(TOK_DEV, KV_HEADS, QH_DEV, HD), axis=2)
        grads_v = jnp.sum(grads_v.reshape(TOK_DEV, KV_HEADS, QH_DEV, HD), axis=2)
        return grads_k.astype(jnp.bfloat16), grads_v.astype(jnp.bfloat16)

    key_parts, value_parts = lax.map(key_block, jnp.arange(block_total, dtype=jnp.int32))
    key_grads = key_parts.reshape(TOKENS, KV_HEADS * HD)
    value_grads = value_parts.reshape(TOKENS, KV_HEADS * HD)
    return query_grads, key_grads, value_grads
```

```python
import functools

import jax
import jax.numpy as jnp
from jax import lax
from jax.experimental import pallas as pl
from jax.experimental.pallas import tpu as pltpu
from jax.sharding import PartitionSpec as P

HD = 128
SOFT_CAP = 50.0
SCORE_SCALE = 1.0 / 12.0
GROUP = 8
LANES = 256
LOG2E = 1.4426950408889634
TANH_SCALE = SCORE_SCALE / SOFT_CAP
EXP_SCALE = SOFT_CAP * LOG2E


def shifted(block, distance):
    count = lax.axis_size("ctx")
    route = [(i, i + distance) for i in range(count) if 0 <= i + distance < count]
    return lax.ppermute(block, "ctx", route)


def document_starts(base, lengths_ref, order_ref, rows, width):
    lane = lax.broadcasted_iota(jnp.int32, (1, width), 1)
    places = base + jnp.where(lane >= rows, lane - rows, lane)
    starts = jnp.zeros((1, width), jnp.int32)
    first = jnp.int32(0)
    bound = jnp.int32(0)
    for i in range(lengths_ref.shape[0]):
        bound = bound + lengths_ref[order_ref[i]]
        starts = jnp.where(bound <= places, bound, starts)
        first = jnp.where(bound <= base, bound, first)
    return starts, first


def transposed_heads(rows_ref, out_ref):
    rows = rows_ref.shape[0]
    for head in range(2):
        out_ref[:, head * rows : (head + 1) * rows] = rows_ref[:, head * HD : (head + 1) * HD].T


def kept(shape, offset, starts, base, rows, diagonal):
    key_row = lax.broadcasted_iota(jnp.int32, shape, 0)
    keep = key_row >= starts - base
    if diagonal:
        lane = lax.broadcasted_iota(jnp.int32, shape, 1) + offset
        keep &= key_row <= jnp.where(lane >= rows, lane - rows, lane)
    return keep


def key_place(base, spot, i, rows):
    return base + (i - spot) * rows - jnp.where(i > spot, GROUP * rows, 0)


def grouped_exchange(blocks):
    count = lax.axis_size("ctx")
    groups = [list(range(g, g + GROUP)) for g in range(0, count, GROUP)]
    return lax.all_to_all(
        blocks, "ctx", split_axis=0, concat_axis=0, axis_index_groups=groups, tiled=True
    )


def dot(a, b):
    return jnp.dot(a, b, preferred_element_type=jnp.float32)


def stats_kernel(
    place_ref, lengths_ref, order_ref, query_ref, window, log_ref, attended_ref, query_t, value_t, starts_ref
):
    rows = query_ref.shape[0]
    width = 2 * rows
    base, spot = place_ref[0], place_ref[1]
    starts, first = document_starts(base, lengths_ref, order_ref, rows, width)
    starts_ref[...] = starts
    transposed_heads(query_ref, query_t)
    log_ref[...] = jnp.zeros_like(log_ref)
    attended_ref[...] = jnp.zeros_like(attended_ref)

    def block(i, diagonal):
        key_base = key_place(base, spot, i, rows)
        value_t[...] = window[i, :, HD:].T
        for c in range(0, width, LANES):
            part = slice(c, c + LANES)
            score = dot(window[i, :, :HD], query_t[:, part])
            expo = jnp.exp2(jnp.tanh(score * TANH_SCALE) * EXP_SCALE)
            keep = kept(expo.shape, c, starts_ref[:, part], key_base, rows, diagonal)
            expo = jnp.where(keep, expo, 0.0)
            log_ref[:, part] += jnp.sum(expo, axis=0, keepdims=True)
            attended_ref[:, part] += dot(value_t[...], expo.astype(jnp.bfloat16))

    block(spot, True)

    def step(j, carry):
        i = lax.rem(spot + j, GROUP)

        @pl.when(key_place(base, spot, i, rows) + rows > first)
        def _():
            block(i, False)

        return carry

    lax.fori_loop(1, GROUP, step, 0)
    attended_ref[...] = attended_ref[...] / log_ref[...]
    log_ref[...] = jnp.log2(log_ref[...])


def grads_kernel(
    place_ref, lengths_ref, order_ref, query_ref, grad_ref, log_ref, attended_ref, window,
    query_grad_ref, own_ref, pieces, query_t, grad_t, query_s, grad_s, key_t, starts_ref, delta_ref, prob_s,
    slope_s, acc,
):
    rows = query_ref.shape[0]
    width = 2 * rows
    base, spot = place_ref[0], place_ref[1]
    starts, first = document_starts(base, lengths_ref, order_ref, rows, width)
    starts_ref[...] = starts
    transposed_heads(query_ref, query_t)
    transposed_heads(grad_ref, grad_t)
    for head in range(2):
        query_s[head * rows : (head + 1) * rows, :] = query_ref[:, head * HD : (head + 1) * HD]
        grad_s[head * rows : (head + 1) * rows, :] = grad_ref[:, head * HD : (head + 1) * HD]
    delta_ref[...] = jnp.sum(
        grad_t[...].astype(jnp.float32) * attended_ref[...], axis=0, keepdims=True
    )
    acc[...] = jnp.zeros_like(acc)

    def block(i, diagonal):
        key_base = key_place(base, spot, i, rows)
        key_t[...] = window[i, :, :HD].T
        for c in range(0, width, LANES):
            part = slice(c, c + LANES)
            score = dot(window[i, :, :HD], query_t[:, part])
            ratio = jnp.tanh(score * TANH_SCALE)
            prob = jnp.exp2(ratio * EXP_SCALE - log_ref[:, part])
            keep = kept(prob.shape, c, starts_ref[:, part], key_base, rows, diagonal)
            prob = jnp.where(keep, prob, 0.0)
            dprob = dot(window[i, :, HD:], grad_t[:, part])
            slope = prob * (dprob - delta_ref[:, part]) * (1.0 - ratio * ratio)
            prob_s[:, part] = prob.astype(jnp.bfloat16)
            slope_s[:, part] = slope.astype(jnp.bfloat16)
        acc[...] += dot(key_t[...], slope_s[...])
        return dot(slope_s[...], query_s[...]) * SCORE_SCALE, dot(prob_s[...], grad_s[...])

    def step(j, carry):
        i = lax.rem(spot + j, GROUP)
        visible = key_place(base, spot, i, rows) + rows > first

        @pl.when(visible)
        def _():
            key_part, value_part = block(i, False)
            pieces[i, :, :HD] = key_part.astype(jnp.bfloat16)
            pieces[i, :, HD:] = value_part.astype(jnp.bfloat16)

        @pl.when(jnp.logical_not(visible))
        def _():
            pieces[i] = jnp.zeros(pieces.shape[1:], jnp.bfloat16)

        return carry

    lax.fori_loop(1, GROUP, step, 0)
    pieces[spot] = jnp.zeros(pieces.shape[1:], jnp.bfloat16)
    key_part, value_part = block(spot, True)
    own_ref[:, :HD] = key_part
    own_ref[:, HD:] = value_part
    for head in range(2):
        query_grad_ref[:, head * HD : (head + 1) * HD] = (
            (acc[:, head * rows : (head + 1) * rows] * SCORE_SCALE).T.astype(jnp.bfloat16)
        )


def smem():
    return pl.BlockSpec(memory_space=pltpu.SMEM)


def vmem():
    return pl.BlockSpec(memory_space=pltpu.VMEM)


def forward_stats(place, doc_lengths, doc_order, query_rows, window):
    rows = query_rows.shape[0]
    width = 2 * rows
    pairs = width * rows * GROUP
    return pl.pallas_call(
        stats_kernel,
        out_shape=(
            jax.ShapeDtypeStruct((1, width), jnp.float32),
            jax.ShapeDtypeStruct((HD, width), jnp.float32),
        ),
        in_specs=[smem()] * 3 + [vmem()] * 2,
        out_specs=(vmem(), vmem()),
        scratch_shapes=[
            pltpu.VMEM((HD, width), jnp.bfloat16),
            pltpu.VMEM((HD, rows), jnp.bfloat16),
            pltpu.VMEM((1, width), jnp.int32),
        ],
        compiler_params=pltpu.CompilerParams(vmem_limit_bytes=32 * 1024 * 1024),
        cost_estimate=pl.CostEstimate(
            flops=4 * pairs * HD, bytes_accessed=4 * 1024 * 1024, transcendentals=2 * pairs
        ),
        name="attention_stats",
    )(place, doc_lengths, doc_order, query_rows, window)


def backward_grads(place, doc_lengths, doc_order, query_rows, head_grads, log_sums, attended, window):
    rows = query_rows.shape[0]
    width = 2 * rows
    pairs = width * rows * GROUP
    return pl.pallas_call(
        grads_kernel,
        out_shape=(
            jax.ShapeDtypeStruct((rows, 2 * HD), jnp.bfloat16),
            jax.ShapeDtypeStruct((rows, 2 * HD), jnp.float32),
            jax.ShapeDtypeStruct((GROUP, rows, 2 * HD), jnp.bfloat16),
        ),
        in_specs=[smem()] * 3 + [vmem()] * 5,
        out_specs=(vmem(),) * 3,
        scratch_shapes=[
            pltpu.VMEM((HD, width), jnp.bfloat16),
            pltpu.VMEM((HD, width), jnp.bfloat16),
            pltpu.VMEM((width, HD), jnp.bfloat16),
            pltpu.VMEM((width, HD), jnp.bfloat16),
            pltpu.VMEM((HD, rows), jnp.bfloat16),
            pltpu.VMEM((1, width), jnp.int32),
            pltpu.VMEM((1, width), jnp.float32),
            pltpu.VMEM((rows, width), jnp.bfloat16),
            pltpu.VMEM((rows, width), jnp.bfloat16),
            pltpu.VMEM((HD, width), jnp.float32),
        ],
        compiler_params=pltpu.CompilerParams(vmem_limit_bytes=32 * 1024 * 1024),
        cost_estimate=pl.CostEstimate(
            flops=10 * pairs * HD, bytes_accessed=8 * 1024 * 1024, transcendentals=2 * pairs
        ),
        name="attention_grads",
    )(place, doc_lengths, doc_order, query_rows, head_grads, log_sums, attended, window)


def on_device(query_rows, key_rows, value_rows, grad_out, out_weight, doc_lengths, doc_order):
    rows = query_rows.shape[0]
    at = lax.axis_index("ctx").astype(jnp.int32)
    spot = lax.rem(at, GROUP)
    place = jnp.stack([at * rows, spot])
    gathered = lax.all_gather(grad_out, "tp", axis=1, tiled=True)
    own_pair = jnp.concatenate([key_rows, value_rows], axis=1)
    before = shifted(own_pair, GROUP)
    slots = jnp.arange(GROUP, dtype=jnp.int32)[:, None, None]
    window = grouped_exchange(jnp.where(slots >= spot, own_pair, before))
    log_sums, attended = forward_stats(place, doc_lengths, doc_order, query_rows, window)
    head_grads = lax.dot_general(
        gathered, out_weight, (((1,), (1,)), ((), ())), preferred_element_type=jnp.float32
    ).astype(jnp.bfloat16)
    query_grads, own, pieces = backward_grads(
        place, doc_lengths, doc_order, query_rows, head_grads, log_sums, attended, window
    )
    returned = grouped_exchange(pieces).astype(jnp.float32)
    for_before = jnp.sum(jnp.where(slots < spot, returned, 0.0), axis=0).astype(jnp.bfloat16)
    own = own + jnp.sum(jnp.where(slots > spot, returned, 0.0), axis=0)
    total = (own + shifted(for_before, -GROUP).astype(jnp.float32)).astype(jnp.bfloat16)
    return query_grads, total[:, :HD], total[:, HD:]


def solution(mesh):
    in_specs = (
        P("ctx", "tp"),
        P("ctx", "tp"),
        P("ctx", "tp"),
        P("ctx", "tp"),
        P("tp", None),
        P(),
        P(),
    )
    out_specs = (P("ctx", "tp"), P("ctx", "tp"), P("ctx", "tp"))
    return jax.shard_map(
        on_device, mesh=mesh, in_specs=in_specs, out_specs=out_specs, check_vma=False
    )
```

```python
import functools

import jax
import jax.numpy as jnp
from jax import lax
from jax.experimental import pallas as pl
from jax.experimental.pallas import tpu as pltpu
from jax.sharding import PartitionSpec as P

HD = 128
SOFT_CAP = 50.0
SCORE_SCALE = 1.0 / 12.0
LANES = 256
LOG2E = 1.4426950408889634
TANH_SCALE = SCORE_SCALE / SOFT_CAP
EXP_SCALE = SOFT_CAP * LOG2E
XS = 4
YS = 4
TASKS = 8
ROW_STEP = 128
VMEM_LIMIT = 48 * 1024 * 1024
HERE, BACK, BACK2, FAR_BACK, FAR = range(5)
SECOND = 5


def permuted(block, axis, target):
    count = lax.axis_size(axis)
    route = [(i, target(i)) for i in range(count) if 0 <= target(i) < count]
    return lax.ppermute(block, axis, route)


def planes_on(block, planes):
    return permuted(block, "ctx", lambda i: i + planes * XS)


def to_query_partner(block):
    return permuted(block, "ctx", lambda i: i ^ 1)


def to_key_partner(block):
    return permuted(block, "ctx", lambda i: i ^ 3)


def to_other_core(block):
    return permuted(block, "tp", lambda i: i ^ 1)


def turned(block, steps):
    return permuted(block, "tp", lambda i: (i + 2 * steps) % (2 * YS))


def dot(a, b):
    return jnp.dot(a, b, preferred_element_type=jnp.float32)


def kept(shape, first_row, offset, starts, key_base, rows, diagonal):
    key_row = lax.broadcasted_iota(jnp.int32, shape, 0) + first_row
    keep = key_row >= starts - key_base
    if diagonal:
        lane = lax.broadcasted_iota(jnp.int32, shape, 1) + offset
        keep &= key_row <= jnp.where(lane >= rows, lane - rows, lane)
    return keep


def load_keys(refs, buffer, semaphores):
    here, back, back2, far = refs
    sources = [here, back, back2, far.at[0], far.at[1]]
    copies = [
        pltpu.make_async_copy(source, buffer.at[i], semaphores.at[i]) for i, source in enumerate(sources)
    ]
    for copy in copies:
        copy.start()
    return copies


def set_queries(base, x, lengths_ref, order_ref, rows, starts_ref):
    width = 2 * rows
    other_base = base + jnp.where(x % 2 == 0, rows, -rows)
    lane = lax.broadcasted_iota(jnp.int32, (1, width), 1)
    lane = jnp.where(lane >= rows, lane - rows, lane)
    bound = jnp.int32(0)
    starts = [jnp.zeros((1, width), jnp.int32)] * 2
    for i in range(lengths_ref.shape[0]):
        bound = bound + lengths_ref[order_ref[i]]
        starts = [
            jnp.where(bound <= place + lane, bound, start) for place, start in zip((base, other_base), starts)
        ]
    starts_ref[:, :width], starts_ref[:, width:] = starts


def task_of(t, base, x, rows):
    even, low = x % 2 == 0, x < 2
    far_base = base + (3 - 2 * x) * rows
    plane = XS * rows
    if t == 0:
        return HERE, base
    if t == 1:
        return jnp.where(even, HERE, BACK2), jnp.where(even, base, base - 2 * plane)
    if t < 4:
        return BACK, base - plane
    if t < 6:
        return FAR_BACK, far_base - plane
    return FAR, jnp.where(low, far_base - 2 * plane, far_base)


def on_lanes(rows_ref, out_ref, at):
    rows = rows_ref.shape[0]
    for head in range(2):
        out_ref[:, at + head * rows : at + (head + 1) * rows] = rows_ref[:, head * HD : (head + 1) * HD].T


def stats_kernel(
    place_ref, lengths_ref, order_ref, query_ref, other_query_ref, here, back, back2, far,
    sums_ref, attended_ref, buffer, query_t, value_t, starts_ref, semaphores,
):
    rows = query_ref.shape[0]
    width = 2 * rows
    copies = load_keys((here, back, back2, far), buffer, semaphores)
    base, x = place_ref[0], place_ref[1]
    set_queries(base, x, lengths_ref, order_ref, rows, starts_ref)
    on_lanes(query_ref, query_t, 0)
    on_lanes(other_query_ref, query_t, width)
    sums_ref[...] = jnp.zeros_like(sums_ref)
    attended_ref[...] = jnp.zeros_like(attended_ref)

    def task(block, key_base, half, diagonal):
        value_t[...] = buffer[block, 1].T
        for c in range(0, width, LANES):
            part = slice(half * width + c, half * width + c + LANES)
            for r in range(0, rows, ROW_STEP):
                score = dot(buffer[block, 0, r : r + ROW_STEP], query_t[:, part])
                expo = jnp.exp2(jnp.tanh(score * TANH_SCALE) * EXP_SCALE)
                keep = kept(expo.shape, r, c, starts_ref[:, part], key_base, rows, diagonal)
                expo = jnp.where(keep, expo, 0.0)
                sums_ref[:, part] += jnp.sum(expo, axis=0, keepdims=True)
                attended_ref[:, part] += dot(value_t[:, r : r + ROW_STEP], expo.astype(jnp.bfloat16))

    for copy in copies:
        copy.wait()
    for t in range(TASKS):
        block, key_base = task_of(t, base, x, rows)
        task(block, key_base, t % 2, t == 0)


def project_kernel(
    place_ref, here, before, after, across_low, across_high, own_weight, other_weight, own_ref, other_ref, across
):
    features = here.shape[0]
    y, core = place_ref[2], place_ref[3]
    across[: features // 2] = across_low[...]
    across[features // 2 :] = across_high[...]
    own = jnp.zeros(own_ref.shape, jnp.float32)
    other = jnp.zeros(own_ref.shape, jnp.float32)
    for steps, block in ((0, here), (YS - 1, before), (1, after), (2, across)):
        at = pl.multiple_of(lax.rem(y + steps, YS) * 2 * features, HD)
        columns = pl.ds(at, 2 * features)

        def of_core(ref):
            return jnp.where(core == 0, ref[:, columns][:, :features], ref[:, columns][:, features:])

        own += dot(of_core(own_weight), block[...])
        other += dot(of_core(other_weight), block[...])
    own_ref[...] = own
    other_ref[...] = other


def delta_kernel(sums_ref, attended_ref, grad_ref, other_grad_ref, out_ref):
    width = attended_ref.shape[1] // 2
    rows = width // 2
    out_ref[0:1, :] = sums_ref[...]
    for i, grads in enumerate((grad_ref, other_grad_ref)):
        for head in range(2):
            at = i * width + head * rows
            lanes = slice(at, at + rows)
            grad = grads[head * HD : (head + 1) * HD, :].astype(jnp.float32)
            out_ref[1:2, lanes] = jnp.sum(grad * attended_ref[:, lanes], axis=0, keepdims=True)
    out_ref[2:, :] = jnp.zeros((6, 2 * width), jnp.float32)


def grads_kernel(
    tasks, slots, place_ref, lengths_ref, order_ref, query_ref, other_query_ref, grad_ref, other_grad_ref,
    stats_ref, other_stats_ref, here, back, back2, far, *refs,
):
    first = FAR in slots
    if first:
        acc, far_ref, refs = refs[0], refs[1], refs[2:]
    else:
        acc_in, query_grad_ref, other_query_grad_ref, here_ref, back_ref, back2_ref, acc, refs = *refs[:7], refs[7:]
    (buffer, query_t, grad_t, query_s, grad_s, key_t, starts_ref, log_ref, delta_ref, prob_s, slope_s, kv_acc,
     semaphores) = refs
    rows = query_ref.shape[0]
    width = 2 * rows
    copies = load_keys((here, back, back2, far), buffer, semaphores)
    base, x = place_ref[0], place_ref[1]
    set_queries(base, x, lengths_ref, order_ref, rows, starts_ref)
    on_lanes(query_ref, query_t, 0)
    on_lanes(other_query_ref, query_t, width)
    for i, (queries, grads) in enumerate(((query_ref, grad_ref), (other_query_ref, other_grad_ref))):
        for head in range(2):
            at = i * width + head * rows
            grad = grads[head * HD : (head + 1) * HD, :]
            grad_t[:, at : at + rows] = grad
            grad_s[at : at + rows, :] = grad.T
            query_s[at : at + rows, :] = queries[:, head * HD : (head + 1) * HD]
        lanes, mirrored = slice(i * width, (i + 1) * width), slice((1 - i) * width, (2 - i) * width)
        total = stats_ref[0:2, lanes] + other_stats_ref[0:2, mirrored]
        log_ref[:, lanes] = jnp.log2(total[0:1])
        delta_ref[:, lanes] = total[1:2] / total[0:1]
    acc[...] = jnp.zeros_like(acc) if first else acc_in[...]
    kv_acc[...] = jnp.zeros_like(kv_acc)

    def pairwise(t):
        block, key_base = task_of(t, base, x, rows)
        half, store = t % 2, t % 2
        key_t[store] = buffer[block, 0].T
        for c in range(0, width, LANES):
            part = slice(half * width + c, half * width + c + LANES)
            score = dot(buffer[block, 0], query_t[:, part])
            ratio = jnp.tanh(score * TANH_SCALE)
            prob = jnp.exp2(ratio * EXP_SCALE - log_ref[:, part])
            keep = kept(prob.shape, 0, c, starts_ref[:, part], key_base, rows, t == 0)
            prob = jnp.where(keep, prob, 0.0)
            dprob = dot(buffer[block, 1], grad_t[:, part])
            slope = prob * (dprob - delta_ref[:, part]) * (1.0 - ratio * ratio)
            prob_s[store, :, c : c + LANES] = prob.astype(jnp.bfloat16)
            slope_s[store, :, c : c + LANES] = slope.astype(jnp.bfloat16)

    def collect(t):
        half, store = t % 2, t % 2
        lanes = slice(half * width, (half + 1) * width)
        out = slots.index((HERE, SECOND, BACK, BACK, FAR_BACK, FAR_BACK, FAR, FAR)[t])
        acc[:, lanes] += dot(key_t[store], slope_s[store])
        kv_acc[out, :, :HD] += dot(slope_s[store], query_s[lanes, :])
        kv_acc[out, :, HD:] += dot(prob_s[store], grad_s[lanes, :])

    for copy in copies:
        copy.wait()
    for t in tasks:
        pairwise(t)
        if t > tasks[0]:
            collect(t - 1)
    collect(tasks[-1])

    def scaled(i):
        return kv_acc[i, :, :HD] * SCORE_SCALE, kv_acc[i, :, HD:]

    if first:
        for i in range(2):
            key_part, value_part = scaled(i)
            far_ref[i, :, :HD] = key_part.astype(jnp.bfloat16)
            far_ref[i, :, HD:] = value_part.astype(jnp.bfloat16)
        return
    even = x % 2 == 0
    back_ref[:, :HD], back_ref[:, HD:] = scaled(slots.index(BACK))
    for i, (own, second) in enumerate(zip(scaled(slots.index(HERE)), scaled(slots.index(SECOND)))):
        here_ref[:, i * HD : (i + 1) * HD] = own + jnp.where(even, second, 0.0)
        back2_ref[:, i * HD : (i + 1) * HD] = jnp.where(even, 0.0, second)
    for head in range(2):
        at = head * rows
        query_grad_ref[:, head * HD : (head + 1) * HD] = (acc[:, at : at + rows] * SCORE_SCALE).T
        at += width
        other_query_grad_ref[:, head * HD : (head + 1) * HD] = (
            (acc[:, at : at + rows] * SCORE_SCALE).T.astype(jnp.bfloat16)
        )


def smem():
    return pl.BlockSpec(memory_space=pltpu.SMEM)


def vmem():
    return pl.BlockSpec(memory_space=pltpu.VMEM)


def hbm():
    return pl.BlockSpec(memory_space=pl.ANY)


def like(shape, dtype):
    return jax.ShapeDtypeStruct(shape, dtype)


def cost(flops, nbytes, transcendentals=0):
    return pl.CostEstimate(flops=flops, bytes_accessed=nbytes, transcendentals=transcendentals)


def params():
    return pltpu.CompilerParams(vmem_limit_bytes=VMEM_LIMIT)


def forward_stats(place, lengths, order, queries, other_queries, keys):
    rows = queries.shape[0]
    width = 2 * rows
    pairs = TASKS * width * rows
    return pl.pallas_call(
        stats_kernel,
        out_shape=(like((1, 2 * width), jnp.float32), like((HD, 2 * width), jnp.float32)),
        in_specs=[smem()] * 3 + [vmem()] * 2 + [hbm()] * 4,
        out_specs=(vmem(),) * 2,
        scratch_shapes=[
            pltpu.VMEM((5, 2, rows, HD), jnp.bfloat16),
            pltpu.VMEM((HD, 2 * width), jnp.bfloat16),
            pltpu.VMEM((HD, rows), jnp.bfloat16),
            pltpu.VMEM((1, 2 * width), jnp.int32),
            pltpu.SemaphoreType.DMA((5,)),
        ],
        compiler_params=params(),
        cost_estimate=cost(4 * pairs * HD, 3_000_000, 2 * pairs),
        name="attention_stats",
    )(place, lengths, order, queries, other_queries, *keys)


def project(place, blocks, own_weight, other_weight):
    heads = own_weight.shape[0]
    features, rows = blocks[0].shape
    return pl.pallas_call(
        project_kernel,
        out_shape=(like((heads, rows), jnp.float32),) * 2,
        in_specs=[smem()] + [vmem()] * 7,
        out_specs=(vmem(),) * 2,
        scratch_shapes=[pltpu.VMEM((features, rows), jnp.bfloat16)],
        compiler_params=params(),
        cost_estimate=cost(4 * YS * heads * rows * features, 5_000_000),
        name="head_projection",
    )(place, *blocks, own_weight, other_weight)


def partial_deltas(sums, attended, grads, other_grads):
    width = attended.shape[1]
    return pl.pallas_call(
        delta_kernel,
        out_shape=like((8, width), jnp.float32),
        in_specs=[vmem()] * 4,
        out_specs=vmem(),
        compiler_params=params(),
        cost_estimate=cost(2 * HD * width, 1_500_000),
        name="partial_deltas",
    )(sums, attended, grads, other_grads)


def backward_grads(place, lengths, order, queries, other_queries, grads, other_grads, stats, other_stats, keys, acc):
    rows = queries.shape[0]
    width = 2 * rows
    first = acc is None
    tasks, slots = ((4, 5, 6, 7), (FAR_BACK, FAR)) if first else ((0, 1, 2, 3), (HERE, SECOND, BACK))
    pairs = len(tasks) * width * rows
    acc_shape = like((HD, 2 * width), jnp.float32)
    block = like((rows, 2 * HD), jnp.float32)
    if first:
        out_shape = (acc_shape, like((2, rows, 2 * HD), jnp.bfloat16))
    else:
        out_shape = (block, like((rows, 2 * HD), jnp.bfloat16), block, block, block)
    return pl.pallas_call(
        functools.partial(grads_kernel, tasks, slots),
        out_shape=out_shape,
        in_specs=[smem()] * 3 + [vmem()] * 6 + [hbm()] * 4 + ([] if first else [vmem()]),
        out_specs=(vmem(),) * len(out_shape),
        scratch_shapes=([] if first else [pltpu.VMEM((HD, 2 * width), jnp.float32)]) + [
            pltpu.VMEM((5, 2, rows, HD), jnp.bfloat16),
            pltpu.VMEM((HD, 2 * width), jnp.bfloat16),
            pltpu.VMEM((HD, 2 * width), jnp.bfloat16),
            pltpu.VMEM((2 * width, HD), jnp.bfloat16),
            pltpu.VMEM((2 * width, HD), jnp.bfloat16),
            pltpu.VMEM((2, HD, rows), jnp.bfloat16),
            pltpu.VMEM((1, 2 * width), jnp.int32),
            pltpu.VMEM((1, 2 * width), jnp.float32),
            pltpu.VMEM((1, 2 * width), jnp.float32),
            pltpu.VMEM((2, rows, width), jnp.bfloat16),
            pltpu.VMEM((2, rows, width), jnp.bfloat16),
            pltpu.VMEM((len(slots), rows, 2 * HD), jnp.float32),
            pltpu.SemaphoreType.DMA((5,)),
        ],
        compiler_params=params(),
        cost_estimate=cost(10 * pairs * HD, 4_000_000, 2 * pairs),
        name="far_grads" if first else "near_grads",
    )(
        place, lengths, order, queries, other_queries, grads, other_grads, stats, other_stats, *keys,
        *(() if first else (acc,)),
    )


def on_device(query_rows, key_rows, value_rows, grad_out, out_weight, doc_lengths, doc_order):
    rows = query_rows.shape[0]
    at = lax.axis_index("ctx").astype(jnp.int32)
    x = lax.rem(at, XS)
    lane = lax.axis_index("tp").astype(jnp.int32)
    core = lax.rem(lane, 2)
    place = jnp.stack([at * rows, x, lane // 2, core])
    features = grad_out.shape[1]

    own = grad_out.T
    before, after = turned(own, 1), turned(own, -1)
    here = jnp.stack([key_rows, value_rows], axis=0)
    back, back2 = planes_on(here, 1), planes_on(here, 2)
    other_queries, other_weight = to_query_partner(query_rows), to_other_core(out_weight)
    before, after, back = lax.optimization_barrier((before, after, back))
    across_low = turned(before[: features // 2], 1)
    across_high = turned(after[features // 2 :], -1)
    far_send = jnp.stack([back, jnp.where(x < 2, here, back2)], axis=0)
    far_send, across_low, across_high = lax.optimization_barrier((far_send, across_low, across_high))
    far = to_key_partner(far_send)
    keys = (here, back, back2, far)

    own_part, other_part = project(
        place, (own, before, after, across_low, across_high), out_weight, other_weight
    )
    grads = (own_part + to_other_core(other_part)).astype(jnp.bfloat16)
    other_grads = to_query_partner(grads)
    sums, attended = forward_stats(place, doc_lengths, doc_order, query_rows, other_queries, keys)
    stats = partial_deltas(sums, attended, grads, other_grads)
    other_stats = to_query_partner(stats)

    common = (
        place, doc_lengths, doc_order, query_rows, other_queries, grads, other_grads, stats, other_stats, keys
    )
    acc, far_grads = backward_grads(*common, None)
    far_grads = to_key_partner(far_grads).astype(jnp.float32)
    query_grads, other_query_grads, here_grads, back_grads, back2_grads = backward_grads(*common, acc)
    other_query_grads = to_query_partner(other_query_grads)
    back2_grads = planes_on(
        (back2_grads + jnp.where(x < 2, 0.0, far_grads[1])).astype(jnp.bfloat16), -2
    )
    back_grads = planes_on((back_grads + far_grads[0]).astype(jnp.bfloat16), -1)
    query_grads = (query_grads + other_query_grads.astype(jnp.float32)).astype(jnp.bfloat16)
    total = here_grads + jnp.where(x < 2, far_grads[1], 0.0)
    total = total + back_grads.astype(jnp.float32) + back2_grads.astype(jnp.float32)
    total = total.astype(jnp.bfloat16)
    return query_grads, total[:, :HD], total[:, HD:]


def solution(mesh):
    in_specs = (
        P("ctx", "tp"),
        P("ctx", "tp"),
        P("ctx", "tp"),
        P("ctx", "tp"),
        P("tp", None),
        P(),
        P(),
    )
    out_specs = (P("ctx", "tp"), P("ctx", "tp"), P("ctx", "tp"))
    return jax.shard_map(
        on_device, mesh=mesh, in_specs=in_specs, out_specs=out_specs, check_vma=False
    )
```

```python
import functools

import jax
import jax.numpy as jnp
from jax import lax
from jax.experimental import pallas as pl
from jax.experimental.pallas import tpu as pltpu
from jax.sharding import PartitionSpec as P

HD = 128
SOFT_CAP = 50.0
SCORE_SCALE = 1.0 / 12.0
LANES = 256
LOG2E = 1.4426950408889634
TANH_SCALE = SCORE_SCALE / SOFT_CAP
EXP_SCALE = SOFT_CAP * LOG2E
XS = 4
YS = 4
TASKS = 8
ROW_STEP = 128
VMEM_LIMIT = 48 * 1024 * 1024
HERE, BACK, BACK2, FAR_BACK, FAR = range(5)
SECOND = 5


def permuted(block, axis, target):
    count = lax.axis_size(axis)
    route = [(i, target(i)) for i in range(count) if 0 <= target(i) < count]
    return lax.ppermute(block, axis, route)


def planes_on(block, planes):
    return permuted(block, "ctx", lambda i: i + planes * XS)


def two_planes_on(block, sign):
    return permuted(block, "ctx", lambda i: i + sign * 2 * XS if i % XS else -1)


def to_query_partner(block):
    return permuted(block, "ctx", lambda i: i ^ 1)


def to_key_partner(block):
    return permuted(block, "ctx", lambda i: i ^ 3)


def to_other_core(block):
    return permuted(block, "tp", lambda i: i ^ 1)


def turned(block, steps):
    return permuted(block, "tp", lambda i: (i + 2 * steps) % (2 * YS))


def dot(a, b):
    return jnp.dot(a, b, preferred_element_type=jnp.float32)


def kept(shape, first_row, offset, starts, key_base, rows, diagonal):
    key_row = lax.broadcasted_iota(jnp.int32, shape, 0) + first_row
    keep = key_row >= starts - key_base
    if diagonal:
        lane = lax.broadcasted_iota(jnp.int32, shape, 1) + offset
        keep &= key_row <= jnp.where(lane >= rows, lane - rows, lane)
    return keep


def load_keys(refs, buffer, semaphores):
    here, back, back2, far = refs
    sources = [here, back, back2, far.at[0], far.at[1]]
    copies = [
        pltpu.make_async_copy(source, buffer.at[i], semaphores.at[i]) for i, source in enumerate(sources)
    ]
    for copy in copies:
        copy.start()
    return copies


def set_queries(base, x, lengths_ref, order_ref, rows, starts_ref):
    width = 2 * rows
    other_base = base + jnp.where(x % 2 == 0, rows, -rows)
    lane = lax.broadcasted_iota(jnp.int32, (1, width), 1)
    lane = jnp.where(lane >= rows, lane - rows, lane)
    bound = jnp.int32(0)
    starts = [jnp.zeros((1, width), jnp.int32)] * 2
    for i in range(lengths_ref.shape[0]):
        bound = bound + lengths_ref[order_ref[i]]
        starts = [
            jnp.where(bound <= place + lane, bound, start) for place, start in zip((base, other_base), starts)
        ]
    starts_ref[:, :width], starts_ref[:, width:] = starts


def task_of(t, base, x, rows):
    even, low = x % 2 == 0, x < 2
    far_base = base + (3 - 2 * x) * rows
    plane = XS * rows
    if t == 0:
        return HERE, base
    if t == 1:
        return jnp.where(even, HERE, BACK2), jnp.where(even, base, base - 2 * plane)
    if t < 4:
        return BACK, base - plane
    if t < 6:
        return FAR_BACK, far_base - plane
    return FAR, jnp.where(low, far_base - 2 * plane, far_base)


def on_lanes(rows_ref, out_ref, at):
    rows = rows_ref.shape[0]
    for head in range(2):
        out_ref[:, at + head * rows : at + (head + 1) * rows] = rows_ref[:, head * HD : (head + 1) * HD].T


def stats_kernel(
    place_ref, lengths_ref, order_ref, query_ref, other_query_ref, here, back, back2, far,
    sums_ref, attended_ref, buffer, query_t, value_t, starts_ref, semaphores,
):
    rows = query_ref.shape[0]
    width = 2 * rows
    copies = load_keys((here, back, back2, far), buffer, semaphores)
    base, x = place_ref[0], place_ref[1]
    set_queries(base, x, lengths_ref, order_ref, rows, starts_ref)
    on_lanes(query_ref, query_t, 0)
    on_lanes(other_query_ref, query_t, width)
    sums_ref[...] = jnp.zeros_like(sums_ref)
    attended_ref[...] = jnp.zeros_like(attended_ref)

    def task(block, key_base, half, diagonal):
        value_t[...] = buffer[block, 1].T
        for c in range(0, width, LANES):
            part = slice(half * width + c, half * width + c + LANES)
            for r in range(0, rows, ROW_STEP):
                score = dot(buffer[block, 0, r : r + ROW_STEP], query_t[:, part])
                expo = jnp.exp2(jnp.tanh(score * TANH_SCALE) * EXP_SCALE)
                keep = kept(expo.shape, r, c, starts_ref[:, part], key_base, rows, diagonal)
                expo = jnp.where(keep, expo, 0.0)
                sums_ref[:, part] += jnp.sum(expo, axis=0, keepdims=True)
                attended_ref[:, part] += dot(value_t[:, r : r + ROW_STEP], expo.astype(jnp.bfloat16))

    for copy in copies:
        copy.wait()
    for t in range(TASKS):
        block, key_base = task_of(t, base, x, rows)
        task(block, key_base, t % 2, t == 0)


def project_kernel(
    place_ref, here, before, after, across_low, across_high, own_weight, other_weight,
    own_ref, other_ref, here_s, across, other_s, semaphores,
):
    here_copy = pltpu.make_async_copy(here, here_s, semaphores.at[0])
    other_copy = pltpu.make_async_copy(other_weight, other_s, semaphores.at[1])
    here_copy.start()
    other_copy.start()
    features = here_s.shape[0]
    y, core = place_ref[2], place_ref[3]
    across[: features // 2] = across_low[...]
    across[features // 2 :] = across_high[...]
    blocks = ((1, after), (2, across), (3, before), (0, here_s))

    def product(weight):
        total = jnp.zeros(own_ref.shape, jnp.float32)
        for steps, block in blocks:
            at = pl.multiple_of(lax.rem(y + steps, YS) * 2 * features, HD)
            both = weight[:, pl.ds(at, 2 * features)]
            total += dot(jnp.where(core == 0, both[:, :features], both[:, features:]), block[...])
        return total

    here_copy.wait()
    own_ref[...] = product(own_weight)
    other_copy.wait()
    other_ref[...] = product(other_s)


def delta_kernel(sums_ref, attended_ref, grad_ref, other_grad_ref, out_ref):
    width = attended_ref.shape[1] // 2
    rows = width // 2
    out_ref[0:1, :] = sums_ref[...]
    for i, grads in enumerate((grad_ref, other_grad_ref)):
        for head in range(2):
            at = i * width + head * rows
            lanes = slice(at, at + rows)
            grad = grads[head * HD : (head + 1) * HD, :].astype(jnp.float32)
            out_ref[1:2, lanes] = jnp.sum(grad * attended_ref[:, lanes], axis=0, keepdims=True)
    out_ref[2:, :] = jnp.zeros((6, 2 * width), jnp.float32)


def grads_kernel(
    tasks, slots, place_ref, lengths_ref, order_ref, query_ref, other_query_ref, grad_ref, other_grad_ref,
    stats_ref, other_stats_ref, here, back, back2, far, *refs,
):
    first = FAR in slots
    if first:
        acc, far_ref, refs = refs[0], refs[1], refs[2:]
    else:
        acc_in, query_grad_ref, other_query_grad_ref, here_ref, back_ref, back2_ref, acc, refs = *refs[:7], refs[7:]
    (buffer, query_t, grad_t, query_s, grad_s, key_t, starts_ref, log_ref, delta_ref, prob_s, slope_s, kv_acc,
     semaphores) = refs
    rows = query_ref.shape[0]
    width = 2 * rows
    copies = load_keys((here, back, back2, far), buffer, semaphores)
    base, x = place_ref[0], place_ref[1]
    set_queries(base, x, lengths_ref, order_ref, rows, starts_ref)
    on_lanes(query_ref, query_t, 0)
    on_lanes(other_query_ref, query_t, width)
    for i, (queries, grads) in enumerate(((query_ref, grad_ref), (other_query_ref, other_grad_ref))):
        for head in range(2):
            at = i * width + head * rows
            grad = grads[head * HD : (head + 1) * HD, :]
            grad_t[:, at : at + rows] = grad
            grad_s[at : at + rows, :] = grad.T
            query_s[at : at + rows, :] = queries[:, head * HD : (head + 1) * HD]
        lanes, mirrored = slice(i * width, (i + 1) * width), slice((1 - i) * width, (2 - i) * width)
        total = stats_ref[0:2, lanes] + other_stats_ref[0:2, mirrored]
        log_ref[:, lanes] = jnp.log2(total[0:1])
        delta_ref[:, lanes] = total[1:2] / total[0:1]
    acc[...] = jnp.zeros_like(acc) if first else acc_in[...]
    kv_acc[...] = jnp.zeros_like(kv_acc)

    def pairwise(t):
        block, key_base = task_of(t, base, x, rows)
        half, store = t % 2, t % 2
        key_t[store] = buffer[block, 0].T
        for c in range(0, width, LANES):
            part = slice(half * width + c, half * width + c + LANES)
            score = dot(buffer[block, 0], query_t[:, part])
            ratio = jnp.tanh(score * TANH_SCALE)
            prob = jnp.exp2(ratio * EXP_SCALE - log_ref[:, part])
            keep = kept(prob.shape, 0, c, starts_ref[:, part], key_base, rows, t == 0)
            prob = jnp.where(keep, prob, 0.0)
            dprob = dot(buffer[block, 1], grad_t[:, part])
            slope = prob * (dprob - delta_ref[:, part]) * (1.0 - ratio * ratio)
            prob_s[store, :, c : c + LANES] = prob.astype(jnp.bfloat16)
            slope_s[store, :, c : c + LANES] = slope.astype(jnp.bfloat16)

    def collect(t):
        half, store = t % 2, t % 2
        lanes = slice(half * width, (half + 1) * width)
        out = slots.index((HERE, SECOND, BACK, BACK, FAR_BACK, FAR_BACK, FAR, FAR)[t])
        acc[:, lanes] += dot(key_t[store], slope_s[store])
        kv_acc[out, :, :HD] += dot(slope_s[store], query_s[lanes, :])
        kv_acc[out, :, HD:] += dot(prob_s[store], grad_s[lanes, :])

    for copy in copies:
        copy.wait()
    for t in tasks:
        pairwise(t)
        if t > tasks[0]:
            collect(t - 1)
    collect(tasks[-1])

    def scaled(i):
        return kv_acc[i, :, :HD] * SCORE_SCALE, kv_acc[i, :, HD:]

    if first:
        for i in range(2):
            key_part, value_part = scaled(i)
            far_ref[i, :, :HD] = key_part.astype(jnp.bfloat16)
            far_ref[i, :, HD:] = value_part.astype(jnp.bfloat16)
        return
    even = x % 2 == 0
    back_ref[:, :HD], back_ref[:, HD:] = scaled(slots.index(BACK))
    for i, (own, second) in enumerate(zip(scaled(slots.index(HERE)), scaled(slots.index(SECOND)))):
        here_ref[:, i * HD : (i + 1) * HD] = own + jnp.where(even, second, 0.0)
        back2_ref[:, i * HD : (i + 1) * HD] = jnp.where(even, 0.0, second)
    for head in range(2):
        at = head * rows
        query_grad_ref[:, head * HD : (head + 1) * HD] = (acc[:, at : at + rows] * SCORE_SCALE).T
        at += width
        other_query_grad_ref[:, head * HD : (head + 1) * HD] = (
            (acc[:, at : at + rows] * SCORE_SCALE).T.astype(jnp.bfloat16)
        )


def smem():
    return pl.BlockSpec(memory_space=pltpu.SMEM)


def vmem():
    return pl.BlockSpec(memory_space=pltpu.VMEM)


def hbm():
    return pl.BlockSpec(memory_space=pl.ANY)


def like(shape, dtype):
    return jax.ShapeDtypeStruct(shape, dtype)


def cost(flops, nbytes, transcendentals=0):
    return pl.CostEstimate(flops=flops, bytes_accessed=nbytes, transcendentals=transcendentals)


def params():
    return pltpu.CompilerParams(vmem_limit_bytes=VMEM_LIMIT)


def forward_stats(place, lengths, order, queries, other_queries, keys):
    rows = queries.shape[0]
    width = 2 * rows
    pairs = TASKS * width * rows
    return pl.pallas_call(
        stats_kernel,
        out_shape=(like((1, 2 * width), jnp.float32), like((HD, 2 * width), jnp.float32)),
        in_specs=[smem()] * 3 + [vmem()] * 2 + [hbm()] * 4,
        out_specs=(vmem(),) * 2,
        scratch_shapes=[
            pltpu.VMEM((5, 2, rows, HD), jnp.bfloat16),
            pltpu.VMEM((HD, 2 * width), jnp.bfloat16),
            pltpu.VMEM((HD, rows), jnp.bfloat16),
            pltpu.VMEM((1, 2 * width), jnp.int32),
            pltpu.SemaphoreType.DMA((5,)),
        ],
        compiler_params=params(),
        cost_estimate=cost(4 * pairs * HD, 3_000_000, 2 * pairs),
        name="attention_stats",
    )(place, lengths, order, queries, other_queries, *keys)


def project(place, blocks, own_weight, other_weight):
    heads = own_weight.shape[0]
    features, rows = blocks[0].shape
    return pl.pallas_call(
        project_kernel,
        out_shape=(like((heads, rows), jnp.float32),) * 2,
        in_specs=[smem(), hbm()] + [vmem()] * 5 + [hbm()],
        out_specs=(vmem(),) * 2,
        scratch_shapes=[
            pltpu.VMEM((features, rows), jnp.bfloat16),
            pltpu.VMEM((features, rows), jnp.bfloat16),
            pltpu.VMEM(own_weight.shape, jnp.bfloat16),
            pltpu.SemaphoreType.DMA((2,)),
        ],
        compiler_params=params(),
        cost_estimate=cost(4 * YS * heads * rows * features, 5_000_000),
        name="head_projection",
    )(place, *blocks, own_weight, other_weight)


def partial_deltas(sums, attended, grads, other_grads):
    width = attended.shape[1]
    return pl.pallas_call(
        delta_kernel,
        out_shape=like((8, width), jnp.float32),
        in_specs=[vmem()] * 4,
        out_specs=vmem(),
        compiler_params=params(),
        cost_estimate=cost(2 * HD * width, 1_500_000),
        name="partial_deltas",
    )(sums, attended, grads, other_grads)


def backward_grads(place, lengths, order, queries, other_queries, grads, other_grads, stats, other_stats, keys, acc):
    rows = queries.shape[0]
    width = 2 * rows
    first = acc is None
    tasks, slots = ((4, 5, 6, 7), (FAR_BACK, FAR)) if first else ((0, 1, 2, 3), (HERE, SECOND, BACK))
    pairs = len(tasks) * width * rows
    acc_shape = like((HD, 2 * width), jnp.float32)
    block = like((rows, 2 * HD), jnp.float32)
    if first:
        out_shape = (acc_shape, like((2, rows, 2 * HD), jnp.bfloat16))
    else:
        out_shape = (block, like((rows, 2 * HD), jnp.bfloat16), block, block, block)
    return pl.pallas_call(
        functools.partial(grads_kernel, tasks, slots),
        out_shape=out_shape,
        in_specs=[smem()] * 3 + [vmem()] * 6 + [hbm()] * 4 + ([] if first else [vmem()]),
        out_specs=(vmem(),) * len(out_shape),
        scratch_shapes=([] if first else [pltpu.VMEM((HD, 2 * width), jnp.float32)]) + [
            pltpu.VMEM((5, 2, rows, HD), jnp.bfloat16),
            pltpu.VMEM((HD, 2 * width), jnp.bfloat16),
            pltpu.VMEM((HD, 2 * width), jnp.bfloat16),
            pltpu.VMEM((2 * width, HD), jnp.bfloat16),
            pltpu.VMEM((2 * width, HD), jnp.bfloat16),
            pltpu.VMEM((2, HD, rows), jnp.bfloat16),
            pltpu.VMEM((1, 2 * width), jnp.int32),
            pltpu.VMEM((1, 2 * width), jnp.float32),
            pltpu.VMEM((1, 2 * width), jnp.float32),
            pltpu.VMEM((2, rows, width), jnp.bfloat16),
            pltpu.VMEM((2, rows, width), jnp.bfloat16),
            pltpu.VMEM((len(slots), rows, 2 * HD), jnp.float32),
            pltpu.SemaphoreType.DMA((5,)),
        ],
        compiler_params=params(),
        cost_estimate=cost(10 * pairs * HD, 4_000_000, 2 * pairs),
        name="far_grads" if first else "near_grads",
    )(
        place, lengths, order, queries, other_queries, grads, other_grads, stats, other_stats, *keys,
        *(() if first else (acc,)),
    )


def on_device(query_rows, key_rows, value_rows, grad_out, out_weight, doc_lengths, doc_order):
    rows = query_rows.shape[0]
    at = lax.axis_index("ctx").astype(jnp.int32)
    x = lax.rem(at, XS)
    lane = lax.axis_index("tp").astype(jnp.int32)
    core = lax.rem(lane, 2)
    place = jnp.stack([at * rows, x, lane // 2, core])
    features = grad_out.shape[1]

    own = grad_out.T
    before, after = turned(own, 1), turned(own, -1)
    here = jnp.stack([key_rows, value_rows], axis=0)
    back, back2 = planes_on(here, 1), two_planes_on(here, 1)
    other_queries = to_query_partner(query_rows)
    other_weight = to_other_core(out_weight)
    before, after, back = lax.optimization_barrier((before, after, back))
    across_low = turned(before[: features // 2], 1)
    across_high = turned(after[features // 2 :], -1)
    far_send = jnp.stack([back, jnp.where(x < 2, here, back2)], axis=0)
    far_send, across_low, across_high = lax.optimization_barrier((far_send, across_low, across_high))
    far = to_key_partner(far_send)
    keys = (here, back, back2, far)

    own_part, other_part = project(
        place, (own, before, after, across_low, across_high), out_weight, other_weight
    )
    grads = (own_part + to_other_core(other_part)).astype(jnp.bfloat16)
    other_grads = to_query_partner(grads)
    sums, attended = forward_stats(place, doc_lengths, doc_order, query_rows, other_queries, keys)
    stats = partial_deltas(sums, attended, grads, other_grads)
    other_stats = to_query_partner(stats)

    common = (
        place, doc_lengths, doc_order, query_rows, other_queries, grads, other_grads, stats, other_stats, keys
    )
    acc, far_grads = backward_grads(*common, None)
    far_grads = to_key_partner(far_grads).astype(jnp.float32)
    query_grads, other_query_grads, here_grads, back_grads, back2_grads = backward_grads(*common, acc)
    other_query_grads = to_query_partner(other_query_grads)
    back2_grads = two_planes_on(
        (back2_grads + jnp.where(x < 2, 0.0, far_grads[1])).astype(jnp.bfloat16), -1
    )
    back_grads = planes_on((back_grads + far_grads[0]).astype(jnp.bfloat16), -1)
    query_grads = (query_grads + other_query_grads.astype(jnp.float32)).astype(jnp.bfloat16)
    total = here_grads + jnp.where(x < 2, far_grads[1], 0.0)
    total = total + back_grads.astype(jnp.float32) + back2_grads.astype(jnp.float32)
    total = total.astype(jnp.bfloat16)
    return query_grads, total[:, :HD], total[:, HD:]


def solution(mesh):
    in_specs = (
        P("ctx", "tp"),
        P("ctx", "tp"),
        P("ctx", "tp"),
        P("ctx", "tp"),
        P("tp", None),
        P(),
        P(),
    )
    out_specs = (P("ctx", "tp"), P("ctx", "tp"), P("ctx", "tp"))
    return jax.shard_map(
        on_device, mesh=mesh, in_specs=in_specs, out_specs=out_specs, check_vma=False
    )
```

```python
import functools

import jax
import jax.numpy as jnp
from jax import lax
from jax.experimental import pallas as pl
from jax.experimental.pallas import tpu as pltpu
from jax.sharding import PartitionSpec as P

HD = 128
SOFT_CAP = 50.0
SCORE_SCALE = 1.0 / 12.0
LANES = 256
LOG2E = 1.4426950408889634
TANH_SCALE = SCORE_SCALE / SOFT_CAP
EXP_SCALE = SOFT_CAP * LOG2E
XS = 4
YS = 4
TASKS = 8
ROW_STEP = 128
VMEM_LIMIT = 48 * 1024 * 1024
HERE, BACK, BACK2, FAR_BACK, FAR = range(5)
SECOND = 5


def permuted(block, axis, target):
    count = lax.axis_size(axis)
    route = [(i, target(i)) for i in range(count) if 0 <= target(i) < count]
    return lax.ppermute(block, axis, route)


def planes_on(block, planes):
    return permuted(block, "ctx", lambda i: i + planes * XS)


def two_planes_on(block):
    return permuted(block, "ctx", lambda i: i + 2 * XS if i % XS else -1)


def from_odd_home(block):
    return permuted(block, "ctx", lambda i: i - 2 * XS if i % 2 else -1)


def far_home(block):
    return permuted(block, "ctx", lambda i: (i ^ 3) - (2 * XS if i % XS < 2 else 0))


def to_query_partner(block):
    return permuted(block, "ctx", lambda i: i ^ 1)


def to_key_partner(block):
    return permuted(block, "ctx", lambda i: i ^ 3)


def to_other_core(block):
    return permuted(block, "tp", lambda i: i ^ 1)


def turned(block, steps):
    return permuted(block, "tp", lambda i: (i + 2 * steps) % (2 * YS))


def dot(a, b):
    return jnp.dot(a, b, preferred_element_type=jnp.float32)


def kept(shape, first_row, offset, starts, key_base, rows, diagonal):
    key_row = lax.broadcasted_iota(jnp.int32, shape, 0) + first_row
    keep = key_row >= starts - key_base
    if diagonal:
        lane = lax.broadcasted_iota(jnp.int32, shape, 1) + offset
        keep &= key_row <= jnp.where(lane >= rows, lane - rows, lane)
    return keep


def load_keys(refs, buffer, semaphores):
    here, back, back2, far = refs
    sources = [here, back, back2, far.at[0], far.at[1]]
    copies = [
        pltpu.make_async_copy(source, buffer.at[i], semaphores.at[i]) for i, source in enumerate(sources)
    ]
    for copy in copies:
        copy.start()
    return copies


def set_queries(base, x, lengths_ref, order_ref, rows, starts_ref):
    width = 2 * rows
    other_base = base + jnp.where(x % 2 == 0, rows, -rows)
    lane = lax.broadcasted_iota(jnp.int32, (1, width), 1)
    lane = jnp.where(lane >= rows, lane - rows, lane)
    bound = jnp.int32(0)
    starts = [jnp.zeros((1, width), jnp.int32)] * 2
    for i in range(lengths_ref.shape[0]):
        bound = bound + lengths_ref[order_ref[i]]
        starts = [
            jnp.where(bound <= place + lane, bound, start) for place, start in zip((base, other_base), starts)
        ]
    starts_ref[:, :width], starts_ref[:, width:] = starts


def task_of(t, base, x, rows):
    even, low = x % 2 == 0, x < 2
    far_base = base + (3 - 2 * x) * rows
    plane = XS * rows
    if t == 0:
        return HERE, base
    if t == 1:
        return jnp.where(even, HERE, BACK2), jnp.where(even, base, base - 2 * plane)
    if t < 4:
        return BACK, base - plane
    if t < 6:
        return FAR_BACK, far_base - plane
    return FAR, jnp.where(low, far_base - 2 * plane, far_base)


def on_lanes(rows_ref, out_ref, at):
    rows = rows_ref.shape[0]
    for head in range(2):
        out_ref[:, at + head * rows : at + (head + 1) * rows] = rows_ref[:, head * HD : (head + 1) * HD].T


def stats_kernel(
    place_ref, lengths_ref, order_ref, query_ref, other_query_ref, here, back, back2, far,
    sums_ref, attended_ref, buffer, query_t, value_t, starts_ref, semaphores,
):
    rows = query_ref.shape[0]
    width = 2 * rows
    copies = load_keys((here, back, back2, far), buffer, semaphores)
    base, x = place_ref[0], place_ref[1]
    set_queries(base, x, lengths_ref, order_ref, rows, starts_ref)
    on_lanes(query_ref, query_t, 0)
    on_lanes(other_query_ref, query_t, width)
    sums_ref[...] = jnp.zeros_like(sums_ref)
    attended_ref[...] = jnp.zeros_like(attended_ref)

    def task(block, key_base, half, diagonal):
        value_t[...] = buffer[block, 1].T
        for c in range(0, width, LANES):
            part = slice(half * width + c, half * width + c + LANES)
            for r in range(0, rows, ROW_STEP):
                score = dot(buffer[block, 0, r : r + ROW_STEP], query_t[:, part])
                expo = jnp.exp2(jnp.tanh(score * TANH_SCALE) * EXP_SCALE)
                keep = kept(expo.shape, r, c, starts_ref[:, part], key_base, rows, diagonal)
                expo = jnp.where(keep, expo, 0.0)
                sums_ref[:, part] += jnp.sum(expo, axis=0, keepdims=True)
                attended_ref[:, part] += dot(value_t[:, r : r + ROW_STEP], expo.astype(jnp.bfloat16))

    for copy in copies:
        copy.wait()
    for t in range(TASKS):
        block, key_base = task_of(t, base, x, rows)
        task(block, key_base, t % 2, t == 0)


def project_kernel(
    place_ref, here, before, after, across_low, across_high, own_weight, other_weight,
    own_ref, other_ref, here_s, across, other_s, semaphores,
):
    here_copy = pltpu.make_async_copy(here, here_s, semaphores.at[0])
    other_copy = pltpu.make_async_copy(other_weight, other_s, semaphores.at[1])
    here_copy.start()
    other_copy.start()
    features = here_s.shape[0]
    y, core = place_ref[2], place_ref[3]
    across[: features // 2] = across_low[...]
    across[features // 2 :] = across_high[...]
    blocks = ((1, after), (2, across), (3, before), (0, here_s))

    def product(weight):
        total = jnp.zeros(own_ref.shape, jnp.float32)
        for steps, block in blocks:
            at = pl.multiple_of(lax.rem(y + steps, YS) * 2 * features, HD)
            both = weight[:, pl.ds(at, 2 * features)]
            total += dot(jnp.where(core == 0, both[:, :features], both[:, features:]), block[...])
        return total

    here_copy.wait()
    own_ref[...] = product(own_weight)
    other_copy.wait()
    other_ref[...] = product(other_s)


def delta_kernel(sums_ref, attended_ref, grad_ref, other_grad_ref, out_ref):
    width = attended_ref.shape[1] // 2
    rows = width // 2
    out_ref[0:1, :] = sums_ref[...]
    for i, grads in enumerate((grad_ref, other_grad_ref)):
        for head in range(2):
            at = i * width + head * rows
            lanes = slice(at, at + rows)
            grad = grads[head * HD : (head + 1) * HD, :].astype(jnp.float32)
            out_ref[1:2, lanes] = jnp.sum(grad * attended_ref[:, lanes], axis=0, keepdims=True)
    out_ref[2:, :] = jnp.zeros((6, 2 * width), jnp.float32)


def grads_kernel(
    tasks, slots, place_ref, lengths_ref, order_ref, query_ref, other_query_ref, grad_ref, other_grad_ref,
    stats_ref, other_stats_ref, here, back, back2, far, *refs,
):
    first = FAR in slots
    if first:
        acc, far_back_ref, far_ref, second_low_ref, second_ref, refs = *refs[:5], refs[5:]
    else:
        acc_in, query_grad_ref, other_query_grad_ref, here_ref, back_ref, acc, refs = *refs[:6], refs[6:]
    (buffer, query_t, grad_t, query_s, grad_s, key_t, starts_ref, log_ref, delta_ref, prob_s, slope_s, kv_acc,
     semaphores) = refs
    rows = query_ref.shape[0]
    width = 2 * rows
    copies = load_keys((here, back, back2, far), buffer, semaphores)
    base, x = place_ref[0], place_ref[1]
    set_queries(base, x, lengths_ref, order_ref, rows, starts_ref)
    on_lanes(query_ref, query_t, 0)
    on_lanes(other_query_ref, query_t, width)
    for i, (queries, grads) in enumerate(((query_ref, grad_ref), (other_query_ref, other_grad_ref))):
        for head in range(2):
            at = i * width + head * rows
            grad = grads[head * HD : (head + 1) * HD, :]
            grad_t[:, at : at + rows] = grad
            grad_s[at : at + rows, :] = grad.T
            query_s[at : at + rows, :] = queries[:, head * HD : (head + 1) * HD]
        lanes, mirrored = slice(i * width, (i + 1) * width), slice((1 - i) * width, (2 - i) * width)
        total = stats_ref[0:2, lanes] + other_stats_ref[0:2, mirrored]
        log_ref[:, lanes] = jnp.log2(total[0:1])
        delta_ref[:, lanes] = total[1:2] / total[0:1]
    acc[...] = jnp.zeros_like(acc) if first else acc_in[...]
    kv_acc[...] = jnp.zeros_like(kv_acc)

    def pairwise(t):
        block, key_base = task_of(t, base, x, rows)
        half, store = t % 2, t % 2
        key_t[store] = buffer[block, 0].T
        for c in range(0, width, LANES):
            part = slice(half * width + c, half * width + c + LANES)
            score = dot(buffer[block, 0], query_t[:, part])
            ratio = jnp.tanh(score * TANH_SCALE)
            prob = jnp.exp2(ratio * EXP_SCALE - log_ref[:, part])
            keep = kept(prob.shape, 0, c, starts_ref[:, part], key_base, rows, t == 0)
            prob = jnp.where(keep, prob, 0.0)
            dprob = dot(buffer[block, 1], grad_t[:, part])
            slope = prob * (dprob - delta_ref[:, part]) * (1.0 - ratio * ratio)
            prob_s[store, :, c : c + LANES] = prob.astype(jnp.bfloat16)
            slope_s[store, :, c : c + LANES] = slope.astype(jnp.bfloat16)

    def collect(t):
        half, store = t % 2, t % 2
        lanes = slice(half * width, (half + 1) * width)
        out = slots.index((HERE, SECOND, BACK, BACK, FAR_BACK, FAR_BACK, FAR, FAR)[t])
        acc[:, lanes] += dot(key_t[store], slope_s[store])
        kv_acc[out, :, :HD] += dot(slope_s[store], query_s[lanes, :])
        kv_acc[out, :, HD:] += dot(prob_s[store], grad_s[lanes, :])

    for copy in copies:
        copy.wait()
    for last, t in zip((None,) + tasks, tasks):
        pairwise(t)
        if last is not None:
            collect(last)
    collect(tasks[-1])

    def scaled(i):
        return kv_acc[i, :, :HD] * SCORE_SCALE, kv_acc[i, :, HD:]

    if first:
        for ref, i in ((far_back_ref, FAR_BACK), (far_ref, FAR), (second_low_ref, SECOND), (second_ref, SECOND)):
            key_part, value_part = scaled(slots.index(i))
            ref[:, :HD], ref[:, HD:] = key_part.astype(ref.dtype), value_part.astype(ref.dtype)
        return
    for ref, i in ((here_ref, HERE), (back_ref, BACK)):
        ref[:, :HD], ref[:, HD:] = scaled(slots.index(i))
    for head in range(2):
        at = head * rows
        query_grad_ref[:, head * HD : (head + 1) * HD] = (acc[:, at : at + rows] * SCORE_SCALE).T
        at += width
        other_query_grad_ref[:, head * HD : (head + 1) * HD] = (
            (acc[:, at : at + rows] * SCORE_SCALE).T.astype(jnp.bfloat16)
        )


def smem():
    return pl.BlockSpec(memory_space=pltpu.SMEM)


def vmem():
    return pl.BlockSpec(memory_space=pltpu.VMEM)


def hbm():
    return pl.BlockSpec(memory_space=pl.ANY)


def like(shape, dtype):
    return jax.ShapeDtypeStruct(shape, dtype)


def cost(flops, nbytes, transcendentals=0):
    return pl.CostEstimate(flops=flops, bytes_accessed=nbytes, transcendentals=transcendentals)


def params():
    return pltpu.CompilerParams(vmem_limit_bytes=VMEM_LIMIT)


def forward_stats(place, lengths, order, queries, other_queries, keys):
    rows = queries.shape[0]
    width = 2 * rows
    pairs = TASKS * width * rows
    return pl.pallas_call(
        stats_kernel,
        out_shape=(like((1, 2 * width), jnp.float32), like((HD, 2 * width), jnp.float32)),
        in_specs=[smem()] * 3 + [vmem()] * 2 + [hbm()] * 4,
        out_specs=(vmem(),) * 2,
        scratch_shapes=[
            pltpu.VMEM((5, 2, rows, HD), jnp.bfloat16),
            pltpu.VMEM((HD, 2 * width), jnp.bfloat16),
            pltpu.VMEM((HD, rows), jnp.bfloat16),
            pltpu.VMEM((1, 2 * width), jnp.int32),
            pltpu.SemaphoreType.DMA((5,)),
        ],
        compiler_params=params(),
        cost_estimate=cost(4 * pairs * HD, 3_000_000, 2 * pairs),
        name="attention_stats",
    )(place, lengths, order, queries, other_queries, *keys)


def project(place, blocks, own_weight, other_weight):
    heads = own_weight.shape[0]
    features, rows = blocks[0].shape
    return pl.pallas_call(
        project_kernel,
        out_shape=(like((heads, rows), jnp.float32),) * 2,
        in_specs=[smem(), hbm()] + [vmem()] * 5 + [hbm()],
        out_specs=(vmem(),) * 2,
        scratch_shapes=[
            pltpu.VMEM((features, rows), jnp.bfloat16),
            pltpu.VMEM((features, rows), jnp.bfloat16),
            pltpu.VMEM(own_weight.shape, jnp.bfloat16),
            pltpu.SemaphoreType.DMA((2,)),
        ],
        compiler_params=params(),
        cost_estimate=cost(4 * YS * heads * rows * features, 5_000_000),
        name="head_projection",
    )(place, *blocks, own_weight, other_weight)


def partial_deltas(sums, attended, grads, other_grads):
    width = attended.shape[1]
    return pl.pallas_call(
        delta_kernel,
        out_shape=like((8, width), jnp.float32),
        in_specs=[vmem()] * 4,
        out_specs=vmem(),
        compiler_params=params(),
        cost_estimate=cost(2 * HD * width, 1_500_000),
        name="partial_deltas",
    )(sums, attended, grads, other_grads)


def backward_grads(place, lengths, order, queries, other_queries, grads, other_grads, stats, other_stats, keys, acc):
    rows = queries.shape[0]
    width = 2 * rows
    first = acc is None
    tasks, slots = ((1, 4, 5, 6, 7), (FAR_BACK, FAR, SECOND)) if first else ((2, 3, 0), (HERE, BACK))
    pairs = len(tasks) * width * rows
    acc_shape = like((HD, 2 * width), jnp.float32)
    wide, block = like((rows, 2 * HD), jnp.float32), like((rows, 2 * HD), jnp.bfloat16)
    out_shape = (acc_shape, block, block, block, wide) if first else (wide, block, wide, wide)
    return pl.pallas_call(
        functools.partial(grads_kernel, tasks, slots),
        out_shape=out_shape,
        in_specs=[smem()] * 3 + [vmem()] * 6 + [hbm()] * 4 + ([] if first else [vmem()]),
        out_specs=(vmem(),) * len(out_shape),
        scratch_shapes=([] if first else [pltpu.VMEM((HD, 2 * width), jnp.float32)]) + [
            pltpu.VMEM((5, 2, rows, HD), jnp.bfloat16),
            pltpu.VMEM((HD, 2 * width), jnp.bfloat16),
            pltpu.VMEM((HD, 2 * width), jnp.bfloat16),
            pltpu.VMEM((2 * width, HD), jnp.bfloat16),
            pltpu.VMEM((2 * width, HD), jnp.bfloat16),
            pltpu.VMEM((2, HD, rows), jnp.bfloat16),
            pltpu.VMEM((1, 2 * width), jnp.int32),
            pltpu.VMEM((1, 2 * width), jnp.float32),
            pltpu.VMEM((1, 2 * width), jnp.float32),
            pltpu.VMEM((2, rows, width), jnp.bfloat16),
            pltpu.VMEM((2, rows, width), jnp.bfloat16),
            pltpu.VMEM((len(slots), rows, 2 * HD), jnp.float32),
            pltpu.SemaphoreType.DMA((5,)),
        ],
        compiler_params=params(),
        cost_estimate=cost(10 * pairs * HD, 4_000_000, 2 * pairs),
        name="far_grads" if first else "near_grads",
    )(
        place, lengths, order, queries, other_queries, grads, other_grads, stats, other_stats, *keys,
        *(() if first else (acc,)),
    )


def on_device(query_rows, key_rows, value_rows, grad_out, out_weight, doc_lengths, doc_order):
    rows = query_rows.shape[0]
    at = lax.axis_index("ctx").astype(jnp.int32)
    x = lax.rem(at, XS)
    lane = lax.axis_index("tp").astype(jnp.int32)
    core = lax.rem(lane, 2)
    place = jnp.stack([at * rows, x, lane // 2, core])
    features = grad_out.shape[1]

    own = grad_out.T
    before, after = turned(own, 1), turned(own, -1)
    here = jnp.stack([key_rows, value_rows], axis=0)
    back, back2 = planes_on(here, 1), two_planes_on(here)
    other_queries = to_query_partner(query_rows)
    other_weight = to_other_core(out_weight)
    before, after, back = lax.optimization_barrier((before, after, back))
    across_low = turned(before[: features // 2], 1)
    across_high = turned(after[features // 2 :], -1)
    far_send = jnp.stack([back, jnp.where(x < 2, here, back2)], axis=0)
    far_send, across_low, across_high = lax.optimization_barrier((far_send, across_low, across_high))
    far = to_key_partner(far_send)
    keys = (here, back, back2, far)

    own_part, other_part = project(
        place, (own, before, after, across_low, across_high), out_weight, other_weight
    )
    grads = (own_part + to_other_core(other_part)).astype(jnp.bfloat16)
    other_grads = to_query_partner(grads)
    sums, attended = forward_stats(place, doc_lengths, doc_order, query_rows, other_queries, keys)
    stats = partial_deltas(sums, attended, grads, other_grads)
    other_stats = to_query_partner(stats)

    common = (
        place, doc_lengths, doc_order, query_rows, other_queries, grads, other_grads, stats, other_stats, keys
    )
    acc, far_back_grads, far_grads, second_low, second = backward_grads(*common, None)
    far_grads, second_low = far_home(far_grads), from_odd_home(second_low)
    far_back_grads = to_key_partner(far_back_grads)
    query_grads, other_query_grads, here_grads, back_grads = backward_grads(*common, acc)
    far_back_grads, far_grads, second_low = lax.optimization_barrier((far_back_grads, far_grads, second_low))
    back_grads = planes_on((back_grads + far_back_grads.astype(jnp.float32)).astype(jnp.bfloat16), -1)
    other_query_grads = to_query_partner(other_query_grads)
    query_grads = (query_grads + other_query_grads.astype(jnp.float32)).astype(jnp.bfloat16)
    total = here_grads + jnp.where(x % 2 == 0, second, 0.0)
    for part in (far_grads, second_low, back_grads):
        total = total + part.astype(jnp.float32)
    total = total.astype(jnp.bfloat16)
    return query_grads, total[:, :HD], total[:, HD:]


def solution(mesh):
    in_specs = (
        P("ctx", "tp"),
        P("ctx", "tp"),
        P("ctx", "tp"),
        P("ctx", "tp"),
        P("tp", None),
        P(),
        P(),
    )
    out_specs = (P("ctx", "tp"), P("ctx", "tp"), P("ctx", "tp"))
    return jax.shard_map(
        on_device, mesh=mesh, in_specs=in_specs, out_specs=out_specs, check_vma=False
    )
```

```python
import functools

import jax
import jax.numpy as jnp
from jax import lax
from jax.experimental import pallas as pl
from jax.experimental.pallas import tpu as pltpu
from jax.sharding import PartitionSpec as P

HD = 128
SOFT_CAP = 50.0
SCORE_SCALE = 1.0 / 12.0
LANES = 256
LOG2E = 1.4426950408889634
TANH_SCALE = SCORE_SCALE / SOFT_CAP
EXP_SCALE = SOFT_CAP * LOG2E
XS = 4
YS = 4
TASKS = 8
ROW_STEP = 128
VMEM_LIMIT = 48 * 1024 * 1024
HERE, BACK, BACK2, FAR_BACK, FAR = range(5)
SECOND = 5


def permuted(block, axis, target):
    count = lax.axis_size(axis)
    route = [(i, target(i)) for i in range(count) if 0 <= target(i) < count]
    return lax.ppermute(block, axis, route)


def planes_on(block, planes):
    return permuted(block, "ctx", lambda i: i + planes * XS)


def two_planes_on(block, sign):
    return permuted(block, "ctx", lambda i: i + sign * 2 * XS if i % XS else -1)


def to_query_partner(block):
    return permuted(block, "ctx", lambda i: i ^ 1)


def to_key_partner(block):
    return permuted(block, "ctx", lambda i: i ^ 3)


def to_other_core(block):
    return permuted(block, "tp", lambda i: i ^ 1)


def turned(block, steps):
    return permuted(block, "tp", lambda i: (i + 2 * steps) % (2 * YS))


def dot(a, b):
    return jnp.dot(a, b, preferred_element_type=jnp.float32)


def kept(shape, first_row, offset, starts, key_base, rows, diagonal):
    key_row = lax.broadcasted_iota(jnp.int32, shape, 0) + first_row
    keep = key_row >= starts - key_base
    if diagonal:
        lane = lax.broadcasted_iota(jnp.int32, shape, 1) + offset
        keep &= key_row <= jnp.where(lane >= rows, lane - rows, lane)
    return keep


def load_keys(refs, buffer, semaphores):
    here, back, back2, far = refs
    sources = [here, back, back2, far.at[0], far.at[1]]
    copies = [
        pltpu.make_async_copy(source, buffer.at[i], semaphores.at[i]) for i, source in enumerate(sources)
    ]
    for copy in copies:
        copy.start()
    return copies


def set_queries(base, x, lengths_ref, order_ref, rows, starts_ref):
    width = 2 * rows
    other_base = base + jnp.where(x % 2 == 0, rows, -rows)
    lane = lax.broadcasted_iota(jnp.int32, (1, width), 1)
    lane = jnp.where(lane >= rows, lane - rows, lane)
    bound = jnp.int32(0)
    starts = [jnp.zeros((1, width), jnp.int32)] * 2
    for i in range(lengths_ref.shape[0]):
        bound = bound + lengths_ref[order_ref[i]]
        starts = [
            jnp.where(bound <= place + lane, bound, start) for place, start in zip((base, other_base), starts)
        ]
    starts_ref[:, :width], starts_ref[:, width:] = starts


def task_of(t, base, x, rows):
    even, low = x % 2 == 0, x < 2
    far_base = base + (3 - 2 * x) * rows
    plane = XS * rows
    if t == 0:
        return HERE, base
    if t == 1:
        return jnp.where(even, HERE, BACK2), jnp.where(even, base, base - 2 * plane)
    if t < 4:
        return BACK, base - plane
    if t < 6:
        return FAR_BACK, far_base - plane
    return FAR, jnp.where(low, far_base - 2 * plane, far_base)


def on_lanes(rows_ref, out_ref, at):
    rows = rows_ref.shape[0]
    for head in range(2):
        out_ref[:, at + head * rows : at + (head + 1) * rows] = rows_ref[:, head * HD : (head + 1) * HD].T


def stats_kernel(
    place_ref, lengths_ref, order_ref, query_ref, other_query_ref, here, back, back2, far,
    sums_ref, attended_ref, buffer, query_t, value_t, starts_ref, semaphores,
):
    rows = query_ref.shape[0]
    width = 2 * rows
    copies = load_keys((here, back, back2, far), buffer, semaphores)
    base, x = place_ref[0], place_ref[1]
    set_queries(base, x, lengths_ref, order_ref, rows, starts_ref)
    on_lanes(query_ref, query_t, 0)
    on_lanes(other_query_ref, query_t, width)
    sums_ref[...] = jnp.zeros_like(sums_ref)
    attended_ref[...] = jnp.zeros_like(attended_ref)

    def task(block, key_base, half, diagonal):
        value_t[...] = buffer[block, 1].T
        for c in range(0, width, LANES):
            part = slice(half * width + c, half * width + c + LANES)
            for r in range(0, rows, ROW_STEP):
                score = dot(buffer[block, 0, r : r + ROW_STEP], query_t[:, part])
                expo = jnp.exp2(jnp.tanh(score * TANH_SCALE) * EXP_SCALE)
                keep = kept(expo.shape, r, c, starts_ref[:, part], key_base, rows, diagonal)
                expo = jnp.where(keep, expo, 0.0)
                sums_ref[:, part] += jnp.sum(expo, axis=0, keepdims=True)
                attended_ref[:, part] += dot(value_t[:, r : r + ROW_STEP], expo.astype(jnp.bfloat16))

    for copy in copies:
        copy.wait()
    for t in range(TASKS):
        block, key_base = task_of(t, base, x, rows)
        task(block, key_base, t % 2, t == 0)


def project_kernel(
    place_ref, here, before, after, across_low, across_high, own_weight, other_weight,
    own_ref, other_ref, here_s, across, other_s, semaphores,
):
    here_copy = pltpu.make_async_copy(here, here_s, semaphores.at[0])
    other_copy = pltpu.make_async_copy(other_weight, other_s, semaphores.at[1])
    here_copy.start()
    other_copy.start()
    features = here_s.shape[0]
    y, core = place_ref[2], place_ref[3]
    across[: features // 2] = across_low[...]
    across[features // 2 :] = across_high[...]
    blocks = ((1, after), (2, across), (3, before), (0, here_s))

    def product(weight):
        total = jnp.zeros(own_ref.shape, jnp.float32)
        for steps, block in blocks:
            at = pl.multiple_of(lax.rem(y + steps, YS) * 2 * features, HD)
            both = weight[:, pl.ds(at, 2 * features)]
            total += dot(jnp.where(core == 0, both[:, :features], both[:, features:]), block[...])
        return total

    here_copy.wait()
    own_ref[...] = product(own_weight)
    other_copy.wait()
    other_ref[...] = product(other_s)


def delta_kernel(sums_ref, attended_ref, grad_ref, other_grad_ref, out_ref):
    width = attended_ref.shape[1] // 2
    rows = width // 2
    out_ref[0:1, :] = sums_ref[...]
    for i, grads in enumerate((grad_ref, other_grad_ref)):
        for head in range(2):
            at = i * width + head * rows
            lanes = slice(at, at + rows)
            grad = grads[head * HD : (head + 1) * HD, :].astype(jnp.float32)
            out_ref[1:2, lanes] = jnp.sum(grad * attended_ref[:, lanes], axis=0, keepdims=True)
    out_ref[2:, :] = jnp.zeros((6, 2 * width), jnp.float32)


def operands_kernel(
    place_ref, lengths_ref, order_ref, query_ref, other_query_ref, grad_ref, other_grad_ref,
    starts_ref, query_t, grad_t, query_s, grad_s,
):
    rows = query_ref.shape[0]
    width = 2 * rows
    set_queries(place_ref[0], place_ref[1], lengths_ref, order_ref, rows, starts_ref)
    on_lanes(query_ref, query_t, 0)
    on_lanes(other_query_ref, query_t, width)
    for i, (queries, grads) in enumerate(((query_ref, grad_ref), (other_query_ref, other_grad_ref))):
        for head in range(2):
            at = i * width + head * rows
            grad = grads[head * HD : (head + 1) * HD, :]
            grad_t[:, at : at + rows] = grad
            grad_s[at : at + rows, :] = grad.T
            query_s[at : at + rows, :] = queries[:, head * HD : (head + 1) * HD]


def grads_kernel(
    tasks, slots, place_ref, starts_ref, query_t, grad_t, query_s, grad_s,
    stats_ref, other_stats_ref, here, back, back2, far, *refs,
):
    first = FAR in slots
    if first:
        acc, far_ref, refs = refs[0], refs[1], refs[2:]
    else:
        acc_in, query_grad_ref, other_query_grad_ref, here_ref, back_ref, back2_ref, acc, refs = *refs[:7], refs[7:]
    buffer, key_t, log_ref, delta_ref, prob_s, slope_s, kv_acc, semaphores = refs
    rows = key_t.shape[2]
    width = 2 * rows
    copies = load_keys((here, back, back2, far), buffer, semaphores)
    base, x = place_ref[0], place_ref[1]
    for i in range(2):
        lanes, mirrored = slice(i * width, (i + 1) * width), slice((1 - i) * width, (2 - i) * width)
        total = stats_ref[0:2, lanes] + other_stats_ref[0:2, mirrored]
        log_ref[:, lanes] = jnp.log2(total[0:1])
        delta_ref[:, lanes] = total[1:2] / total[0:1]
    acc[...] = jnp.zeros_like(acc) if first else acc_in[...]
    kv_acc[...] = jnp.zeros_like(kv_acc)

    def pairwise(t):
        block, key_base = task_of(t, base, x, rows)
        half, store = t % 2, t % 2
        key_t[store] = buffer[block, 0].T
        for c in range(0, width, LANES):
            part = slice(half * width + c, half * width + c + LANES)
            score = dot(buffer[block, 0], query_t[:, part])
            ratio = jnp.tanh(score * TANH_SCALE)
            prob = jnp.exp2(ratio * EXP_SCALE - log_ref[:, part])
            keep = kept(prob.shape, 0, c, starts_ref[:, part], key_base, rows, t == 0)
            prob = jnp.where(keep, prob, 0.0)
            dprob = dot(buffer[block, 1], grad_t[:, part])
            slope = prob * (dprob - delta_ref[:, part]) * (1.0 - ratio * ratio)
            prob_s[store, :, c : c + LANES] = prob.astype(jnp.bfloat16)
            slope_s[store, :, c : c + LANES] = slope.astype(jnp.bfloat16)

    def collect(t):
        half, store = t % 2, t % 2
        lanes = slice(half * width, (half + 1) * width)
        out = slots.index((HERE, SECOND, BACK, BACK, FAR_BACK, FAR_BACK, FAR, FAR)[t])
        acc[:, lanes] += dot(key_t[store], slope_s[store])
        kv_acc[out, :, :HD] += dot(slope_s[store], query_s[lanes, :])
        kv_acc[out, :, HD:] += dot(prob_s[store], grad_s[lanes, :])

    for copy in copies:
        copy.wait()
    for t in tasks:
        pairwise(t)
        if t > tasks[0]:
            collect(t - 1)
    collect(tasks[-1])

    def scaled(i):
        return kv_acc[i, :, :HD] * SCORE_SCALE, kv_acc[i, :, HD:]

    if first:
        for i in range(2):
            key_part, value_part = scaled(i)
            far_ref[i, :, :HD] = key_part.astype(jnp.bfloat16)
            far_ref[i, :, HD:] = value_part.astype(jnp.bfloat16)
        return
    even = x % 2 == 0
    back_ref[:, :HD], back_ref[:, HD:] = scaled(slots.index(BACK))
    for i, (own, second) in enumerate(zip(scaled(slots.index(HERE)), scaled(slots.index(SECOND)))):
        here_ref[:, i * HD : (i + 1) * HD] = own + jnp.where(even, second, 0.0)
        back2_ref[:, i * HD : (i + 1) * HD] = jnp.where(even, 0.0, second)
    for head in range(2):
        at = head * rows
        query_grad_ref[:, head * HD : (head + 1) * HD] = (acc[:, at : at + rows] * SCORE_SCALE).T
        at += width
        other_query_grad_ref[:, head * HD : (head + 1) * HD] = (
            (acc[:, at : at + rows] * SCORE_SCALE).T.astype(jnp.bfloat16)
        )


def smem():
    return pl.BlockSpec(memory_space=pltpu.SMEM)


def vmem():
    return pl.BlockSpec(memory_space=pltpu.VMEM)


def hbm():
    return pl.BlockSpec(memory_space=pl.ANY)


def like(shape, dtype):
    return jax.ShapeDtypeStruct(shape, dtype)


def cost(flops, nbytes, transcendentals=0):
    return pl.CostEstimate(flops=flops, bytes_accessed=nbytes, transcendentals=transcendentals)


def params():
    return pltpu.CompilerParams(vmem_limit_bytes=VMEM_LIMIT)


def forward_stats(place, lengths, order, queries, other_queries, keys):
    rows = queries.shape[0]
    width = 2 * rows
    pairs = TASKS * width * rows
    return pl.pallas_call(
        stats_kernel,
        out_shape=(like((1, 2 * width), jnp.float32), like((HD, 2 * width), jnp.float32)),
        in_specs=[smem()] * 3 + [vmem()] * 2 + [hbm()] * 4,
        out_specs=(vmem(),) * 2,
        scratch_shapes=[
            pltpu.VMEM((5, 2, rows, HD), jnp.bfloat16),
            pltpu.VMEM((HD, 2 * width), jnp.bfloat16),
            pltpu.VMEM((HD, rows), jnp.bfloat16),
            pltpu.VMEM((1, 2 * width), jnp.int32),
            pltpu.SemaphoreType.DMA((5,)),
        ],
        compiler_params=params(),
        cost_estimate=cost(4 * pairs * HD, 3_000_000, 2 * pairs),
        name="attention_stats",
    )(place, lengths, order, queries, other_queries, *keys)


def project(place, blocks, own_weight, other_weight):
    heads = own_weight.shape[0]
    features, rows = blocks[0].shape
    return pl.pallas_call(
        project_kernel,
        out_shape=(like((heads, rows), jnp.float32),) * 2,
        in_specs=[smem(), hbm()] + [vmem()] * 5 + [hbm()],
        out_specs=(vmem(),) * 2,
        scratch_shapes=[
            pltpu.VMEM((features, rows), jnp.bfloat16),
            pltpu.VMEM((features, rows), jnp.bfloat16),
            pltpu.VMEM(own_weight.shape, jnp.bfloat16),
            pltpu.SemaphoreType.DMA((2,)),
        ],
        compiler_params=params(),
        cost_estimate=cost(4 * YS * heads * rows * features, 5_000_000),
        name="head_projection",
    )(place, *blocks, own_weight, other_weight)


def partial_deltas(sums, attended, grads, other_grads):
    width = attended.shape[1]
    return pl.pallas_call(
        delta_kernel,
        out_shape=like((8, width), jnp.float32),
        in_specs=[vmem()] * 4,
        out_specs=vmem(),
        compiler_params=params(),
        cost_estimate=cost(2 * HD * width, 1_500_000),
        name="partial_deltas",
    )(sums, attended, grads, other_grads)


def gradient_operands(place, lengths, order, queries, other_queries, grads, other_grads):
    rows = queries.shape[0]
    width = 2 * rows
    return pl.pallas_call(
        operands_kernel,
        out_shape=(like((1, 2 * width), jnp.int32),)
        + (like((HD, 2 * width), jnp.bfloat16),) * 2
        + (like((2 * width, HD), jnp.bfloat16),) * 2,
        in_specs=[smem()] * 3 + [vmem()] * 4,
        out_specs=(vmem(),) * 5,
        compiler_params=params(),
        cost_estimate=cost(8 * HD * width, 2_400_000),
        name="gradient_operands",
    )(place, lengths, order, queries, other_queries, grads, other_grads)


def backward_grads(place, operands, stats, other_stats, keys, acc):
    width = operands[0].shape[1] // 2
    rows = width // 2
    first = acc is None
    tasks, slots = ((4, 5, 6, 7), (FAR_BACK, FAR)) if first else ((0, 1, 2, 3), (HERE, SECOND, BACK))
    pairs = len(tasks) * width * rows
    acc_shape = like((HD, 2 * width), jnp.float32)
    block = like((rows, 2 * HD), jnp.float32)
    if first:
        out_shape = (acc_shape, like((2, rows, 2 * HD), jnp.bfloat16))
    else:
        out_shape = (block, like((rows, 2 * HD), jnp.bfloat16), block, block, block)
    return pl.pallas_call(
        functools.partial(grads_kernel, tasks, slots),
        out_shape=out_shape,
        in_specs=[smem()] + [vmem()] * 7 + [hbm()] * 4 + ([] if first else [vmem()]),
        out_specs=(vmem(),) * len(out_shape),
        scratch_shapes=([] if first else [pltpu.VMEM((HD, 2 * width), jnp.float32)]) + [
            pltpu.VMEM((5, 2, rows, HD), jnp.bfloat16),
            pltpu.VMEM((2, HD, rows), jnp.bfloat16),
            pltpu.VMEM((1, 2 * width), jnp.float32),
            pltpu.VMEM((1, 2 * width), jnp.float32),
            pltpu.VMEM((2, rows, width), jnp.bfloat16),
            pltpu.VMEM((2, rows, width), jnp.bfloat16),
            pltpu.VMEM((len(slots), rows, 2 * HD), jnp.float32),
            pltpu.SemaphoreType.DMA((5,)),
        ],
        compiler_params=params(),
        cost_estimate=cost(10 * pairs * HD, 4_000_000, 2 * pairs),
        name="far_grads" if first else "near_grads",
    )(
        place, *operands, stats, other_stats, *keys, *(() if first else (acc,)),
    )


def on_device(query_rows, key_rows, value_rows, grad_out, out_weight, doc_lengths, doc_order):
    rows = query_rows.shape[0]
    at = lax.axis_index("ctx").astype(jnp.int32)
    x = lax.rem(at, XS)
    lane = lax.axis_index("tp").astype(jnp.int32)
    core = lax.rem(lane, 2)
    place = jnp.stack([at * rows, x, lane // 2, core])
    features = grad_out.shape[1]

    own = grad_out.T
    before, after = turned(own, 1), turned(own, -1)
    here = jnp.stack([key_rows, value_rows], axis=0)
    back, back2 = planes_on(here, 1), two_planes_on(here, 1)
    other_queries = to_query_partner(query_rows)
    other_weight = to_other_core(out_weight)
    before, after, back = lax.optimization_barrier((before, after, back))
    across_low = turned(before[: features // 2], 1)
    across_high = turned(after[features // 2 :], -1)
    far_send = jnp.stack([back, jnp.where(x < 2, here, back2)], axis=0)
    far_send, across_low, across_high = lax.optimization_barrier((far_send, across_low, across_high))
    far = to_key_partner(far_send)
    keys = (here, back, back2, far)

    own_part, other_part = project(
        place, (own, before, after, across_low, across_high), out_weight, other_weight
    )
    grads = (own_part + to_other_core(other_part)).astype(jnp.bfloat16)
    other_grads = to_query_partner(grads)
    sums, attended = forward_stats(place, doc_lengths, doc_order, query_rows, other_queries, keys)
    stats = partial_deltas(sums, attended, grads, other_grads)
    other_stats = to_query_partner(stats)

    operands = gradient_operands(
        place, doc_lengths, doc_order, query_rows, other_queries, grads, other_grads
    )
    common = (place, operands, stats, other_stats, keys)
    acc, far_grads = backward_grads(*common, None)
    far_grads = to_key_partner(far_grads).astype(jnp.float32)
    query_grads, other_query_grads, here_grads, back_grads, back2_grads = backward_grads(*common, acc)
    other_query_grads = to_query_partner(other_query_grads)
    back2_grads = two_planes_on(
        (back2_grads + jnp.where(x < 2, 0.0, far_grads[1])).astype(jnp.bfloat16), -1
    )
    back_grads = planes_on((back_grads + far_grads[0]).astype(jnp.bfloat16), -1)
    query_grads = (query_grads + other_query_grads.astype(jnp.float32)).astype(jnp.bfloat16)
    total = here_grads + jnp.where(x < 2, far_grads[1], 0.0)
    total = total + back_grads.astype(jnp.float32) + back2_grads.astype(jnp.float32)
    total = total.astype(jnp.bfloat16)
    return query_grads, total[:, :HD], total[:, HD:]


def solution(mesh):
    in_specs = (
        P("ctx", "tp"),
        P("ctx", "tp"),
        P("ctx", "tp"),
        P("ctx", "tp"),
        P("tp", None),
        P(),
        P(),
    )
    out_specs = (P("ctx", "tp"), P("ctx", "tp"), P("ctx", "tp"))
    return jax.shard_map(
        on_device, mesh=mesh, in_specs=in_specs, out_specs=out_specs, check_vma=False
    )
```

```python
import functools

import jax
import jax.numpy as jnp
from jax import lax
from jax.experimental import pallas as pl
from jax.experimental.pallas import tpu as pltpu
from jax.sharding import PartitionSpec as P

HD = 128
SOFT_CAP = 50.0
SCORE_SCALE = 1.0 / 12.0
LANES = 256
LOG2E = 1.4426950408889634
TANH_SCALE = SCORE_SCALE / SOFT_CAP
EXP_SCALE = SOFT_CAP * LOG2E
XS = 4
YS = 4
TASKS = 8
ROW_STEP = 128
VMEM_LIMIT = 48 * 1024 * 1024
HERE, BACK, BACK2, FAR_BACK, FAR = range(5)
SECOND = 5


def permuted(block, axis, target):
    count = lax.axis_size(axis)
    route = [(i, target(i)) for i in range(count) if 0 <= target(i) < count]
    return lax.ppermute(block, axis, route)


def planes_on(block, planes):
    return permuted(block, "ctx", lambda i: i + planes * XS)


def two_planes_on(block, sign):
    return permuted(block, "ctx", lambda i: i + sign * 2 * XS if i % XS else -1)


def to_query_partner(block):
    return permuted(block, "ctx", lambda i: i ^ 1)


def to_key_partner(block):
    return permuted(block, "ctx", lambda i: i ^ 3)


def to_other_core(block):
    return permuted(block, "tp", lambda i: i ^ 1)


def turned(block, steps):
    return permuted(block, "tp", lambda i: (i + 2 * steps) % (2 * YS))


def dot(a, b):
    return jnp.dot(a, b, preferred_element_type=jnp.float32)


def kept(shape, first_row, offset, starts, key_base, rows, diagonal):
    key_row = lax.broadcasted_iota(jnp.int32, shape, 0) + first_row
    keep = key_row >= starts - key_base
    if diagonal:
        lane = lax.broadcasted_iota(jnp.int32, shape, 1) + offset
        keep &= key_row <= jnp.where(lane >= rows, lane - rows, lane)
    return keep


BLOCKS_OF = ((HERE,), (HERE, BACK2), (BACK,), (BACK,), (FAR_BACK,), (FAR_BACK,), (FAR,), (FAR,))


def load_keys(refs, buffer, semaphores, tasks):
    here, back, back2, far = refs
    sources = (here, back, back2, far.at[0], far.at[1])
    pending = {}
    for t in tasks:
        for i in BLOCKS_OF[t]:
            if i not in pending:
                pending[i] = pltpu.make_async_copy(sources[i], buffer.at[i], semaphores.at[i])
                pending[i].start()
    return pending


def wait_keys(pending, t):
    for i in BLOCKS_OF[t]:
        if i in pending:
            pending.pop(i).wait()


def set_queries(base, x, lengths_ref, order_ref, rows, starts_ref):
    width = 2 * rows
    other_base = base + jnp.where(x % 2 == 0, rows, -rows)
    lane = lax.broadcasted_iota(jnp.int32, (1, width), 1)
    lane = jnp.where(lane >= rows, lane - rows, lane)
    bound = jnp.int32(0)
    starts = [jnp.zeros((1, width), jnp.int32)] * 2
    for i in range(lengths_ref.shape[0]):
        bound = bound + lengths_ref[order_ref[i]]
        starts = [
            jnp.where(bound <= place + lane, bound, start) for place, start in zip((base, other_base), starts)
        ]
    starts_ref[:, :width], starts_ref[:, width:] = starts


def task_of(t, base, x, rows):
    even, low = x % 2 == 0, x < 2
    far_base = base + (3 - 2 * x) * rows
    plane = XS * rows
    if t == 0:
        return HERE, base
    if t == 1:
        return jnp.where(even, HERE, BACK2), jnp.where(even, base, base - 2 * plane)
    if t < 4:
        return BACK, base - plane
    if t < 6:
        return FAR_BACK, far_base - plane
    return FAR, jnp.where(low, far_base - 2 * plane, far_base)


def on_lanes(rows_ref, out_ref, at):
    rows = rows_ref.shape[0]
    for head in range(2):
        out_ref[:, at + head * rows : at + (head + 1) * rows] = rows_ref[:, head * HD : (head + 1) * HD].T


def stats_kernel(
    place_ref, lengths_ref, order_ref, query_ref, other_query_ref, here, back, back2, far,
    sums_ref, attended_ref, buffer, query_t, value_t, starts_ref, semaphores,
):
    rows = query_ref.shape[0]
    width = 2 * rows
    pending = load_keys((here, back, back2, far), buffer, semaphores, range(TASKS))
    base, x = place_ref[0], place_ref[1]
    set_queries(base, x, lengths_ref, order_ref, rows, starts_ref)
    on_lanes(query_ref, query_t, 0)
    on_lanes(other_query_ref, query_t, width)
    sums_ref[...] = jnp.zeros_like(sums_ref)
    attended_ref[...] = jnp.zeros_like(attended_ref)

    def task(block, key_base, half, diagonal):
        value_t[...] = buffer[block, 1].T
        for c in range(0, width, LANES):
            part = slice(half * width + c, half * width + c + LANES)
            for r in range(0, rows, ROW_STEP):
                score = dot(buffer[block, 0, r : r + ROW_STEP], query_t[:, part])
                expo = jnp.exp2(jnp.tanh(score * TANH_SCALE) * EXP_SCALE)
                keep = kept(expo.shape, r, c, starts_ref[:, part], key_base, rows, diagonal)
                expo = jnp.where(keep, expo, 0.0)
                sums_ref[:, part] += jnp.sum(expo, axis=0, keepdims=True)
                attended_ref[:, part] += dot(value_t[:, r : r + ROW_STEP], expo.astype(jnp.bfloat16))

    for t in range(TASKS):
        wait_keys(pending, t)
        block, key_base = task_of(t, base, x, rows)
        task(block, key_base, t % 2, t == 0)


def project_kernel(
    place_ref, here, before, after, across_low, across_high, own_weight, other_weight,
    own_ref, other_ref, here_s, across, other_s, semaphores,
):
    here_copy = pltpu.make_async_copy(here, here_s, semaphores.at[0])
    other_copy = pltpu.make_async_copy(other_weight, other_s, semaphores.at[1])
    here_copy.start()
    other_copy.start()
    features = here_s.shape[0]
    y, core = place_ref[2], place_ref[3]
    across[: features // 2] = across_low[...]
    across[features // 2 :] = across_high[...]
    blocks = ((1, after), (2, across), (3, before), (0, here_s))

    def product(weight):
        total = jnp.zeros(own_ref.shape, jnp.float32)
        for steps, block in blocks:
            at = pl.multiple_of(lax.rem(y + steps, YS) * 2 * features, HD)
            both = weight[:, pl.ds(at, 2 * features)]
            total += dot(jnp.where(core == 0, both[:, :features], both[:, features:]), block[...])
        return total

    here_copy.wait()
    own_ref[...] = product(own_weight)
    other_copy.wait()
    other_ref[...] = product(other_s)


def delta_kernel(sums_ref, attended_ref, grad_ref, other_grad_ref, out_ref):
    width = attended_ref.shape[1] // 2
    rows = width // 2
    out_ref[0:1, :] = sums_ref[...]
    for i, grads in enumerate((grad_ref, other_grad_ref)):
        for head in range(2):
            at = i * width + head * rows
            lanes = slice(at, at + rows)
            grad = grads[head * HD : (head + 1) * HD, :].astype(jnp.float32)
            out_ref[1:2, lanes] = jnp.sum(grad * attended_ref[:, lanes], axis=0, keepdims=True)
    out_ref[2:, :] = jnp.zeros((6, 2 * width), jnp.float32)


def operands_kernel(
    place_ref, lengths_ref, order_ref, query_ref, other_query_ref, grad_ref, other_grad_ref,
    starts_ref, query_t, grad_t, query_s, grad_s,
):
    rows = query_ref.shape[0]
    width = 2 * rows
    set_queries(place_ref[0], place_ref[1], lengths_ref, order_ref, rows, starts_ref)
    on_lanes(query_ref, query_t, 0)
    on_lanes(other_query_ref, query_t, width)
    for i, (queries, grads) in enumerate(((query_ref, grad_ref), (other_query_ref, other_grad_ref))):
        for head in range(2):
            at = i * width + head * rows
            grad = grads[head * HD : (head + 1) * HD, :]
            grad_t[:, at : at + rows] = grad
            grad_s[at : at + rows, :] = grad.T
            query_s[at : at + rows, :] = queries[:, head * HD : (head + 1) * HD]


def grads_kernel(
    tasks, slots, place_ref, starts_ref, query_t, grad_t, query_s, grad_s,
    stats_ref, other_stats_ref, here, back, back2, far, *refs,
):
    first = FAR in slots
    if first:
        acc, far_ref, refs = refs[0], refs[1], refs[2:]
    else:
        acc_in, query_grad_ref, other_query_grad_ref, here_ref, back_ref, back2_ref, acc, refs = *refs[:7], refs[7:]
    buffer, key_t, log_ref, delta_ref, prob_s, slope_s, kv_acc, semaphores = refs
    rows = key_t.shape[2]
    width = 2 * rows
    pending = load_keys((here, back, back2, far), buffer, semaphores, tasks)
    base, x = place_ref[0], place_ref[1]
    for i in range(2):
        lanes, mirrored = slice(i * width, (i + 1) * width), slice((1 - i) * width, (2 - i) * width)
        total = stats_ref[0:2, lanes] + other_stats_ref[0:2, mirrored]
        log_ref[:, lanes] = jnp.log2(total[0:1])
        delta_ref[:, lanes] = total[1:2] / total[0:1]
    acc[...] = jnp.zeros_like(acc) if first else acc_in[...]
    kv_acc[...] = jnp.zeros_like(kv_acc)

    def pairwise(t):
        block, key_base = task_of(t, base, x, rows)
        half, store = t % 2, t % 2
        key_t[store] = buffer[block, 0].T
        for c in range(0, width, LANES):
            part = slice(half * width + c, half * width + c + LANES)
            score = dot(buffer[block, 0], query_t[:, part])
            ratio = jnp.tanh(score * TANH_SCALE)
            prob = jnp.exp2(ratio * EXP_SCALE - log_ref[:, part])
            keep = kept(prob.shape, 0, c, starts_ref[:, part], key_base, rows, t == 0)
            prob = jnp.where(keep, prob, 0.0)
            dprob = dot(buffer[block, 1], grad_t[:, part])
            slope = prob * (dprob - delta_ref[:, part]) * (1.0 - ratio * ratio)
            prob_s[store, :, c : c + LANES] = prob.astype(jnp.bfloat16)
            slope_s[store, :, c : c + LANES] = slope.astype(jnp.bfloat16)

    def collect(t):
        half, store = t % 2, t % 2
        lanes = slice(half * width, (half + 1) * width)
        out = slots.index((HERE, SECOND, BACK, BACK, FAR_BACK, FAR_BACK, FAR, FAR)[t])
        acc[:, lanes] += dot(key_t[store], slope_s[store])
        kv_acc[out, :, :HD] += dot(slope_s[store], query_s[lanes, :])
        kv_acc[out, :, HD:] += dot(prob_s[store], grad_s[lanes, :])

    for t in tasks:
        wait_keys(pending, t)
        pairwise(t)
        if t > tasks[0]:
            collect(t - 1)
    collect(tasks[-1])

    def scaled(i):
        return kv_acc[i, :, :HD] * SCORE_SCALE, kv_acc[i, :, HD:]

    if first:
        for i in range(2):
            key_part, value_part = scaled(i)
            far_ref[i, :, :HD] = key_part.astype(jnp.bfloat16)
            far_ref[i, :, HD:] = value_part.astype(jnp.bfloat16)
        return
    even = x % 2 == 0
    back_ref[:, :HD], back_ref[:, HD:] = scaled(slots.index(BACK))
    for i, (own, second) in enumerate(zip(scaled(slots.index(HERE)), scaled(slots.index(SECOND)))):
        here_ref[:, i * HD : (i + 1) * HD] = own + jnp.where(even, second, 0.0)
        back2_ref[:, i * HD : (i + 1) * HD] = jnp.where(even, 0.0, second)
    for head in range(2):
        at = head * rows
        query_grad_ref[:, head * HD : (head + 1) * HD] = (acc[:, at : at + rows] * SCORE_SCALE).T
        at += width
        other_query_grad_ref[:, head * HD : (head + 1) * HD] = (
            (acc[:, at : at + rows] * SCORE_SCALE).T.astype(jnp.bfloat16)
        )


def smem():
    return pl.BlockSpec(memory_space=pltpu.SMEM)


def vmem():
    return pl.BlockSpec(memory_space=pltpu.VMEM)


def hbm():
    return pl.BlockSpec(memory_space=pl.ANY)


def like(shape, dtype):
    return jax.ShapeDtypeStruct(shape, dtype)


def cost(flops, nbytes, transcendentals=0):
    return pl.CostEstimate(flops=flops, bytes_accessed=nbytes, transcendentals=transcendentals)


def params():
    return pltpu.CompilerParams(vmem_limit_bytes=VMEM_LIMIT)


def forward_stats(place, lengths, order, queries, other_queries, keys):
    rows = queries.shape[0]
    width = 2 * rows
    pairs = TASKS * width * rows
    return pl.pallas_call(
        stats_kernel,
        out_shape=(like((1, 2 * width), jnp.float32), like((HD, 2 * width), jnp.float32)),
        in_specs=[smem()] * 3 + [vmem()] * 2 + [hbm()] * 4,
        out_specs=(vmem(),) * 2,
        scratch_shapes=[
            pltpu.VMEM((5, 2, rows, HD), jnp.bfloat16),
            pltpu.VMEM((HD, 2 * width), jnp.bfloat16),
            pltpu.VMEM((HD, rows), jnp.bfloat16),
            pltpu.VMEM((1, 2 * width), jnp.int32),
            pltpu.SemaphoreType.DMA((5,)),
        ],
        compiler_params=params(),
        cost_estimate=cost(4 * pairs * HD, 3_000_000, 2 * pairs),
        name="attention_stats",
    )(place, lengths, order, queries, other_queries, *keys)


def project(place, blocks, own_weight, other_weight):
    heads = own_weight.shape[0]
    features, rows = blocks[0].shape
    return pl.pallas_call(
        project_kernel,
        out_shape=(like((heads, rows), jnp.float32),) * 2,
        in_specs=[smem(), hbm()] + [vmem()] * 5 + [hbm()],
        out_specs=(vmem(),) * 2,
        scratch_shapes=[
            pltpu.VMEM((features, rows), jnp.bfloat16),
            pltpu.VMEM((features, rows), jnp.bfloat16),
            pltpu.VMEM(own_weight.shape, jnp.bfloat16),
            pltpu.SemaphoreType.DMA((2,)),
        ],
        compiler_params=params(),
        cost_estimate=cost(4 * YS * heads * rows * features, 5_000_000),
        name="head_projection",
    )(place, *blocks, own_weight, other_weight)


def partial_deltas(sums, attended, grads, other_grads):
    width = attended.shape[1]
    return pl.pallas_call(
        delta_kernel,
        out_shape=like((8, width), jnp.float32),
        in_specs=[vmem()] * 4,
        out_specs=vmem(),
        compiler_params=params(),
        cost_estimate=cost(2 * HD * width, 1_500_000),
        name="partial_deltas",
    )(sums, attended, grads, other_grads)


def gradient_operands(place, lengths, order, queries, other_queries, grads, other_grads):
    rows = queries.shape[0]
    width = 2 * rows
    return pl.pallas_call(
        operands_kernel,
        out_shape=(like((1, 2 * width), jnp.int32),)
        + (like((HD, 2 * width), jnp.bfloat16),) * 2
        + (like((2 * width, HD), jnp.bfloat16),) * 2,
        in_specs=[smem()] * 3 + [vmem()] * 4,
        out_specs=(vmem(),) * 5,
        compiler_params=params(),
        cost_estimate=cost(8 * HD * width, 2_400_000),
        name="gradient_operands",
    )(place, lengths, order, queries, other_queries, grads, other_grads)


def backward_grads(place, operands, stats, other_stats, keys, acc):
    width = operands[0].shape[1] // 2
    rows = width // 2
    first = acc is None
    tasks, slots = ((4, 5, 6, 7), (FAR_BACK, FAR)) if first else ((0, 1, 2, 3), (HERE, SECOND, BACK))
    pairs = len(tasks) * width * rows
    acc_shape = like((HD, 2 * width), jnp.float32)
    block = like((rows, 2 * HD), jnp.float32)
    if first:
        out_shape = (acc_shape, like((2, rows, 2 * HD), jnp.bfloat16))
    else:
        out_shape = (block, like((rows, 2 * HD), jnp.bfloat16), block, block, block)
    return pl.pallas_call(
        functools.partial(grads_kernel, tasks, slots),
        out_shape=out_shape,
        in_specs=[smem()] + [vmem()] * 7 + [hbm()] * 4 + ([] if first else [vmem()]),
        out_specs=(vmem(),) * len(out_shape),
        scratch_shapes=([] if first else [pltpu.VMEM((HD, 2 * width), jnp.float32)]) + [
            pltpu.VMEM((5, 2, rows, HD), jnp.bfloat16),
            pltpu.VMEM((2, HD, rows), jnp.bfloat16),
            pltpu.VMEM((1, 2 * width), jnp.float32),
            pltpu.VMEM((1, 2 * width), jnp.float32),
            pltpu.VMEM((2, rows, width), jnp.bfloat16),
            pltpu.VMEM((2, rows, width), jnp.bfloat16),
            pltpu.VMEM((len(slots), rows, 2 * HD), jnp.float32),
            pltpu.SemaphoreType.DMA((5,)),
        ],
        compiler_params=params(),
        cost_estimate=cost(10 * pairs * HD, 4_000_000, 2 * pairs),
        name="far_grads" if first else "near_grads",
    )(
        place, *operands, stats, other_stats, *keys, *(() if first else (acc,)),
    )


def on_device(query_rows, key_rows, value_rows, grad_out, out_weight, doc_lengths, doc_order):
    rows = query_rows.shape[0]
    at = lax.axis_index("ctx").astype(jnp.int32)
    x = lax.rem(at, XS)
    lane = lax.axis_index("tp").astype(jnp.int32)
    core = lax.rem(lane, 2)
    place = jnp.stack([at * rows, x, lane // 2, core])
    features = grad_out.shape[1]

    own = grad_out.T
    before, after = turned(own, 1), turned(own, -1)
    here = jnp.stack([key_rows, value_rows], axis=0)
    back, back2 = planes_on(here, 1), two_planes_on(here, 1)
    other_queries = to_query_partner(query_rows)
    other_weight = to_other_core(out_weight)
    before, after, back = lax.optimization_barrier((before, after, back))
    across_low = turned(before[: features // 2], 1)
    across_high = turned(after[features // 2 :], -1)
    far_send = jnp.stack([back, jnp.where(x < 2, here, back2)], axis=0)
    far_send, across_low, across_high = lax.optimization_barrier((far_send, across_low, across_high))
    far = to_key_partner(far_send)
    keys = (here, back, back2, far)

    own_part, other_part = project(
        place, (own, before, after, across_low, across_high), out_weight, other_weight
    )
    grads = (own_part + to_other_core(other_part)).astype(jnp.bfloat16)
    other_grads = to_query_partner(grads)
    sums, attended = forward_stats(place, doc_lengths, doc_order, query_rows, other_queries, keys)
    stats = partial_deltas(sums, attended, grads, other_grads)
    other_stats = to_query_partner(stats)

    operands = gradient_operands(
        place, doc_lengths, doc_order, query_rows, other_queries, grads, other_grads
    )
    common = (place, operands, stats, other_stats, keys)
    acc, far_grads = backward_grads(*common, None)
    far_grads = to_key_partner(far_grads).astype(jnp.float32)
    query_grads, other_query_grads, here_grads, back_grads, back2_grads = backward_grads(*common, acc)
    other_query_grads = to_query_partner(other_query_grads)
    back2_grads = two_planes_on(
        (back2_grads + jnp.where(x < 2, 0.0, far_grads[1])).astype(jnp.bfloat16), -1
    )
    back_grads = planes_on((back_grads + far_grads[0]).astype(jnp.bfloat16), -1)
    query_grads = (query_grads + other_query_grads.astype(jnp.float32)).astype(jnp.bfloat16)
    total = here_grads + jnp.where(x < 2, far_grads[1], 0.0)
    total = total + back_grads.astype(jnp.float32) + back2_grads.astype(jnp.float32)
    total = total.astype(jnp.bfloat16)
    return query_grads, total[:, :HD], total[:, HD:]


def solution(mesh):
    in_specs = (
        P("ctx", "tp"),
        P("ctx", "tp"),
        P("ctx", "tp"),
        P("ctx", "tp"),
        P("tp", None),
        P(),
        P(),
    )
    out_specs = (P("ctx", "tp"), P("ctx", "tp"), P("ctx", "tp"))
    return jax.shard_map(
        on_device, mesh=mesh, in_specs=in_specs, out_specs=out_specs, check_vma=False
    )
```
